128 devices in a mesh: pipe: 8 (over y_lo, z), expert: 16 (over y_hi, x, core).
Axes of the slice: x: 4, y: 4 (y_hi: 2, y_lo: 2; y = y_hi * 2 + y_lo), z: 4, core: 2. Of those that a mesh axis runs over, the one named last changes fastest.
Arguments:
- saved_input: bfloat16 [8, 3072, 7168], P('pipe', 'expert'), may hold values from -6 to 6
- grad_output: bfloat16 [8, 3072, 7168], P('pipe', 'expert'), may hold values from -6 to 6
- routes: int32 [8, 3072, 8], P('pipe', 'expert'), may hold values from 0 to 255, as said below
- route_weight: float32 [8, 3072, 8], P('pipe', 'expert'), may hold values from 0.2 to 1
- gate_weight: bfloat16 [8, 7168, 4096], P('pipe', None, 'expert'), may hold values from -0.0625 to 0.0625
- up_weight: bfloat16 [8, 7168, 4096], P('pipe', None, 'expert'), may hold values from -0.0625 to 0.0625
- down_weight: bfloat16 [8, 4096, 7168], P('pipe', 'expert'), may hold values from -0.125 to 0.125
- mirror_grad: bfloat16 [8, 4096, 7168], P('pipe', 'expert'), may hold values from -6 to 6
Outputs:
- next_cotangent: bfloat16 [8, 3072, 7168], P('pipe', 'expert')
- down_grad: bfloat16 [8, 4096, 7168], P('pipe', 'expert')
The draws below stay inside these ranges and needn't reach their ends.
Inputs may be any that keep to these rules, and one draw needn't show every extreme that they name: `routes`: each token names 8 different experts; the window holds experts 0 to 1. Of the 192 tokens of one device (one section, aligned blocks of 192 tokens), at most 24 name any one window expert; in each section some window expert is named by exactly 24 tokens of every block.
All inputs are finite; a program needn't handle non-finite values.
Results may differ from the reference program's by a relative error of at most 0.0057.
Values may be sent and summed in bfloat16 or wider, within the bound.
No kernel may reach another device: no remote copies, remote signals or barrier semaphores. Data moves between devices by JAX's collectives and lax.ppermute only.
A program may use at most 128 MiB of HBM per device.

```python
import jax
import jax.numpy as jnp
from jax import lax

D = 7168
FF = 2048
ROUTED = 256
TOPK = 8
HID_DEV = 256
TOK_DEV = 192
SPLIT = 8
EXP_WIN = 2
CAP = 24
TOKENS = 3072
SECTIONS = 8
N_EXPERT = 16


def draw_routes(key, part):
    key = jax.random.fold_in(key, 7)
    keys = jax.random.split(key, 5)
    counts = jax.random.randint(keys[0], (SECTIONS, N_EXPERT, EXP_WIN), CAP // 3, CAP + 1)
    fullest = jax.random.randint(keys[1], (SECTIONS, 1, 1), 0, EXP_WIN)
    counts = jnp.where(jnp.arange(EXP_WIN)[None, None, :] == fullest, CAP, counts)
    order_keys = jax.random.randint(keys[2], (SECTIONS, N_EXPERT, EXP_WIN, TOK_DEV), 0, 2 ** 20) * TOK_DEV + jnp.arange(TOK_DEV)
    positions = jnp.argsort(jnp.argsort(order_keys, axis=-1), axis=-1)
    member = positions < counts[..., None]
    window_scores = jnp.where(member, 2 ** 29 + jnp.arange(EXP_WIN)[:, None], -1)
    window_scores = jnp.transpose(window_scores, (0, 1, 3, 2))
    other_scores = jax.random.randint(keys[3], (SECTIONS, N_EXPERT, TOK_DEV, ROUTED - EXP_WIN), 0, 2 ** 20) * ROUTED + jnp.arange(ROUTED - EXP_WIN)
    scores = jnp.concatenate([window_scores, other_scores], axis=-1).astype(jnp.int32)
    chosen = lax.top_k(scores, TOPK)[1].astype(jnp.int32)
    column_keys = jax.random.randint(keys[4], (SECTIONS, N_EXPERT, TOK_DEV, TOPK), 0, 2 ** 20) * TOPK + jnp.arange(TOPK)
    shuffle = jnp.argsort(column_keys, axis=-1)
    shuffled = jnp.take_along_axis(chosen, shuffle, axis=-1)
    return shuffled.reshape(SECTIONS, N_EXPERT * TOK_DEV, TOPK).astype(jnp.int32)


def block_scale(key, shape, cuts, least, high):
    gain = 1.0
    for axis_at, blocks in cuts:
        draws = jax.random.uniform(jax.random.fold_in(jax.random.fold_in(key, 6), axis_at), (blocks,), jnp.float32, least / len(cuts), high / len(cuts))
        gain = gain * jnp.repeat(jnp.exp(draws), shape[axis_at] // blocks).reshape((-1,) + (1,) * (len(shape) - 1 - axis_at))
    return gain


def centred(rng, dims, width, reach, pieces=(), kind=jnp.bfloat16):
    factor_of = block_scale(rng, dims, pieces, -0.22, 0.18) if pieces else 1.0
    entries = jax.random.normal(rng, dims, jnp.float32) * width * factor_of
    return jnp.minimum(jnp.maximum(entries, -reach), reach).astype(kind)


def setup_inputs(seed: int = 0) -> dict:
    seeds = jax.random.split(jax.random.key(seed), 9)
    return {
        "saved_input": centred(seeds[0], (SECTIONS, TOKENS, D), 1.0, 6.0, ((0, 8), (1, 16))),
        "grad_output": centred(seeds[1], (SECTIONS, TOKENS, D), 1.0, 6.0, ((0, 8), (1, 16))),
        "routes": draw_routes(jax.random.fold_in(seeds[8], 71), 0),
        "route_weight": jnp.clip(0.2 + 0.8 * jax.random.uniform(seeds[3], (SECTIONS, TOKENS, TOPK), jnp.float32) ** block_scale(seeds[3], (SECTIONS, TOKENS, TOPK), ((0, 8), (1, 16)), -0.2, 0.2), 0.2, 1.0),
        "gate_weight": centred(seeds[4], (SECTIONS, D, EXP_WIN * FF), D ** -0.5, 0.0625, ((0, 8), (2, 16))),
        "up_weight": centred(seeds[5], (SECTIONS, D, EXP_WIN * FF), D ** -0.5, 0.0625, ((0, 8), (2, 16))),
        "down_weight": centred(seeds[6], (SECTIONS, EXP_WIN * FF, D), FF ** -0.5, 0.125, ((0, 8), (1, 16))),
        "mirror_grad": centred(seeds[7], (SECTIONS, EXP_WIN * FF, D), 1.0, 6.0, ((0, 8), (1, 16))),
    }


def section_backward(inputs, cotangent, chosen, weights, gate_part, up_part, down_part):
    total_rows = N_EXPERT * CAP
    cotangent_f = cotangent.astype(jnp.float32)
    total = jnp.zeros((TOKENS, D), jnp.float32)
    blocks = []
    for expert_id in range(EXP_WIN):
        matches = chosen == expert_id
        member = jnp.any(matches, axis=-1)
        scale = jnp.sum(jnp.where(matches, weights, jnp.float32(0.0)), axis=-1)
        flags = member.reshape(N_EXPERT, TOK_DEV).astype(jnp.int32)
        slot_index = jnp.cumsum(flags, axis=1).astype(jnp.int32) - 1
        row_index = jnp.arange(N_EXPERT, dtype=jnp.int32)[:, None] * CAP + slot_index
        row_index = jnp.where(flags == 1, row_index, total_rows).reshape(TOKENS).astype(jnp.int32)
        scaled = (scale[:, None] * cotangent_f).astype(jnp.bfloat16)
        expert_rows = jnp.zeros((total_rows, D), jnp.bfloat16).at[row_index].set(inputs, mode="drop")
        scaled_rows = jnp.zeros((total_rows, D), jnp.bfloat16).at[row_index].set(scaled, mode="drop")
        lower = expert_id * FF
        gate_cols = gate_part[:, lower:lower + FF]
        up_cols = up_part[:, lower:lower + FF]
        down_rows = down_part[lower:lower + FF, :]
        pre_gate = jnp.dot(expert_rows, gate_cols, preferred_element_type=jnp.float32)
        pre_up = jnp.dot(expert_rows, up_cols, preferred_element_type=jnp.float32)
        from_down = jnp.dot(scaled_rows, down_rows.T, preferred_element_type=jnp.float32)
        sigma = jax.nn.sigmoid(pre_gate)
        activated = pre_gate * sigma
        hidden = (activated * pre_up).astype(jnp.bfloat16)
        slope = sigma * (1.0 + pre_gate * (1.0 - sigma))
        grad_gate = (from_down * pre_up * slope).astype(jnp.bfloat16)
        grad_up = (from_down * activated).astype(jnp.bfloat16)
        partial_sum = jnp.zeros((total_rows, D), jnp.float32)
        for block_index in range(SPLIT):
            start = block_index * HID_DEV
            stop = start + HID_DEV
            piece = jnp.dot(grad_gate[:, start:stop], gate_cols[:, start:stop].T, preferred_element_type=jnp.float32)
            piece = piece + jnp.dot(grad_up[:, start:stop], up_cols[:, start:stop].T, preferred_element_type=jnp.float32)
            rounded = lax.optimization_barrier(piece.astype(jnp.bfloat16))
            partial_sum = partial_sum + rounded.astype(jnp.float32)
        total = total + jnp.take(partial_sum, row_index, axis=0, mode="fill", fill_value=0.0)
        blocks.append(jnp.dot(hidden.T, scaled_rows, preferred_element_type=jnp.float32))
    back = (cotangent_f + total).astype(jnp.bfloat16)
    return back, jnp.concatenate(blocks, axis=0)


def reference(saved_input, grad_output, routes, route_weight, gate_weight, up_weight, down_weight, mirror_grad):
    def one_section(section_index):
        return section_backward(saved_input[section_index], grad_output[section_index], routes[section_index],
                              route_weight[section_index], gate_weight[section_index], up_weight[section_index],
                              down_weight[section_index])

    back, local = lax.map(one_section, jnp.arange(SECTIONS, dtype=jnp.int32))
    next_cotangent = jnp.roll(back, -1, axis=0)
    down_grad = (local + mirror_grad[::-1].astype(jnp.float32)).astype(jnp.bfloat16)
    return next_cotangent, down_grad
```

```python
import functools

import jax
import jax.numpy as jnp
from jax import lax
from jax.experimental import pallas as pl
from jax.experimental.pallas import tpu as pltpu
from jax.sharding import PartitionSpec as P

CAP = 24
BLOCK = 1024
LIMIT = 48 * 1024 * 1024
F32 = jnp.float32
BF16 = jnp.bfloat16

BEHIND = [(i, (i - 1) % 8) for i in range(8)]
MIRROR = [(i, 7 - i) for i in range(8)]
ODD_BEHIND = [(i, i - 1) for i in range(1, 8, 2)]
AWAY_FIRST = [(0, 2), (2, 0), (4, 6), (6, 4)]
AWAY_LAST = [(2, 7), (6, 3), (0, 1), (4, 5)]
ACROSS = [(i, i ^ 8) for i in range(16)]
SIBLING = [(i, i ^ 1) for i in range(16)]


def along_x(by):
    return [(i, (i // 8) * 8 + ((i // 2 + by) % 4) * 2 + i % 2) for i in range(16)]


OFFSETS = (1, 3, 2)


def params(**kw):
    return pltpu.CompilerParams(vmem_limit_bytes=LIMIT, **kw)


def cost(flops, nbytes):
    return pl.CostEstimate(flops=flops, bytes_accessed=nbytes, transcendentals=0)


def one_hot_rows(plane, routes):
    tokens = routes.shape[1]
    chosen = routes[...]
    line = lax.broadcasted_iota(jnp.int32, (2 * CAP, tokens), 0)
    member = jnp.zeros((2 * CAP, tokens), F32)
    for j in range(2):
        expert = plane[0] if j == 0 else 1 - plane[0]
        named = jnp.max(jnp.where(chosen == expert, 1.0, 0.0), axis=0, keepdims=True)
        member = jnp.where(line >= CAP if j else line < CAP, named, member)
    row = lax.broadcasted_iota(jnp.int32, (tokens, tokens), 0)
    column = lax.broadcasted_iota(jnp.int32, (tokens, tokens), 1)
    upper = jnp.where(row <= column, 1.0, 0.0).astype(BF16)
    count = jnp.dot(member.astype(BF16), upper, preferred_element_type=F32)
    slot = jnp.where(line >= CAP, line - CAP, line).astype(F32)
    return jnp.where((count - 1.0 == slot) & (member > 0.0), 1.0, 0.0)


def pick_body(plane, routes, weight, saved, grad, own, other, first, second, one_hot, gain):
    tokens = routes.shape[1]

    @pl.when(pl.program_id(0) == 0)
    def _():
        hot = one_hot_rows(plane, routes)
        line = lax.broadcasted_iota(jnp.int32, (2 * CAP, tokens), 0)
        scale = jnp.zeros((2 * CAP, tokens), F32)
        for j in range(2):
            expert = plane[0] if j == 0 else 1 - plane[0]
            value = jnp.where(routes[...] == expert, weight[...], 0.0)
            value = jnp.sum(value, axis=0, keepdims=True)
            scale = jnp.where(line >= CAP if j else line < CAP, value, scale)
        one_hot[...] = hot.astype(BF16)
        total = jnp.sum(hot * scale, axis=1, keepdims=True)
        gain[...] = jnp.broadcast_to(total, gain.shape)

    pick = one_hot[...]
    grads = grad[...]
    rows = jnp.dot(pick, saved[...], preferred_element_type=F32)
    scaled = gain[:, :1] * jnp.dot(pick, grads, preferred_element_type=F32)
    own[...] = jnp.concatenate([rows[:CAP], scaled[:CAP]], axis=0).astype(BF16)
    other[...] = jnp.concatenate([rows[CAP:], scaled[CAP:]], axis=0).astype(BF16)
    first[...] = grads[: tokens // 2]
    second[...] = grads[tokens // 2 :]


def pick_rows(plane, routes, weight, saved, grad):
    tokens, depth = saved.shape
    whole = pl.BlockSpec(routes.shape, lambda k: (0, 0))
    tall = pl.BlockSpec((tokens, BLOCK), lambda k: (0, k))
    short = pl.BlockSpec((2 * CAP, BLOCK), lambda k: (0, k))
    half = pl.BlockSpec((tokens // 2, BLOCK), lambda k: (0, k))
    rows = jax.ShapeDtypeStruct((2 * CAP, depth), BF16)
    halves = jax.ShapeDtypeStruct((tokens // 2, depth), BF16)
    return pl.pallas_call(
        pick_body,
        grid=(depth // BLOCK,),
        in_specs=[pl.BlockSpec(memory_space=pltpu.SMEM), whole, whole, tall, tall],
        out_specs=[short, short, half, half],
        out_shape=[rows, rows, halves, halves],
        scratch_shapes=[pltpu.VMEM((2 * CAP, tokens), BF16), pltpu.VMEM((2 * CAP, 128), F32)],
        compiler_params=params(),
        cost_estimate=cost(4 * 48 * tokens * depth, 10 * tokens * depth),
        name="pick_rows",
    )(plane, routes, weight, saved, grad)


def stacked(refs, lower):
    parts = [ref[...].astype(F32)[lower : lower + CAP] for ref in refs]
    return jnp.concatenate(parts, axis=0).astype(BF16)


def contract_last(a, b):
    return lax.dot_general(a, b, (((1,), (1,)), ((), ())), preferred_element_type=F32)


def experts_body(steps, *refs):
    arrivals, (gate, up, down) = refs[:8], refs[8:11]
    mine, sibling, sibling_2, hidden_t = refs[11:15]
    gates, ups, pre_gate, pre_up, from_down, grad_gate, grad_up = refs[15:]
    step = pl.program_id(0)

    @pl.when(step == 0)
    def _():
        pre_gate[...] = jnp.zeros_like(pre_gate)
        pre_up[...] = jnp.zeros_like(pre_up)
        from_down[...] = jnp.zeros_like(from_down)

    @pl.when(step < steps)
    def _():
        rows = stacked(arrivals, 0)
        scaled = stacked(arrivals, CAP)
        gates[step] = gate[...]
        ups[step] = up[...]
        pre_gate[...] += jnp.dot(rows, gate[...], preferred_element_type=F32)
        pre_up[...] += jnp.dot(rows, up[...], preferred_element_type=F32)
        from_down[...] += contract_last(scaled, down[...])

    @pl.when(step == steps)
    def _():
        value = pre_gate[...]
        sigma = 1.0 / (1.0 + jnp.exp(-value))
        activated = value * sigma
        slope = sigma * (1.0 + value * (1.0 - sigma))
        hidden_t[...] = (activated * pre_up[...]).T.astype(BF16)
        grad_gate[...] = (from_down[...] * pre_up[...] * slope).astype(BF16)
        grad_up[...] = (from_down[...] * activated).astype(BF16)

    @pl.when(step >= steps)
    def _():
        at = step - steps
        partial = contract_last(grad_gate[...], gates[at])
        partial = (partial + contract_last(grad_up[...], ups[at])).astype(BF16)
        half = partial.shape[0] // 2
        mine[...] = partial[:half]
        sibling[...] = partial[half : half + half // 2]
        sibling_2[...] = partial[half + half // 2 :]


def experts(arrivals, gate, up, down):
    depth, width = gate.shape
    steps = depth // BLOCK
    count = 8 * CAP

    def block(k):
        return jnp.minimum(k, steps - 1)

    def late(k):
        return jnp.maximum(k - steps, 0)

    out = pl.BlockSpec((count // 2, BLOCK), lambda k: (0, late(k)))
    half = pl.BlockSpec((count // 4, BLOCK), lambda k: (0, late(k)))
    sums = jax.ShapeDtypeStruct((count // 2, depth), BF16)
    halves = jax.ShapeDtypeStruct((count // 4, depth), BF16)
    return pl.pallas_call(
        functools.partial(experts_body, steps),
        grid=(2 * steps,),
        in_specs=[pl.BlockSpec((2 * CAP, BLOCK), lambda k: (0, block(k)))] * 8
        + [pl.BlockSpec((BLOCK, width), lambda k: (block(k), 0))] * 2
        + [pl.BlockSpec((width, BLOCK), lambda k: (0, block(k)))],
        out_specs=[out, half, half, pl.BlockSpec((width, count), lambda k: (0, 0))],
        out_shape=[sums, halves, halves, jax.ShapeDtypeStruct((width, count), BF16)],
        scratch_shapes=[pltpu.VMEM((steps, BLOCK, width), BF16)] * 2
        + [pltpu.VMEM((count, width), F32)] * 3
        + [pltpu.VMEM((count, width), BF16)] * 2,
        compiler_params=params(),
        cost_estimate=cost(10 * count * depth * width, 2 * depth * (3 * width + 3 * count)),
        name="experts",
    )(*arrivals, gate, up, down)


def split_body(mine, first, second, *outs):
    theirs = jnp.concatenate([first[...].astype(F32), second[...].astype(F32)], axis=0)
    total = mine[...].astype(F32) + theirs
    for i, out in enumerate(outs):
        out[...] = total[i * CAP : (i + 1) * CAP].astype(BF16)


def split_sum(mine, first, second):
    count, depth = mine.shape
    spec = pl.BlockSpec((count, BLOCK), lambda k: (0, k))
    half = pl.BlockSpec((count // 2, BLOCK), lambda k: (0, k))
    out = pl.BlockSpec((CAP, BLOCK), lambda k: (0, k))
    return pl.pallas_call(
        split_body,
        grid=(depth // BLOCK,),
        in_specs=[spec, half, half],
        out_specs=[out] * 4,
        out_shape=[jax.ShapeDtypeStruct((CAP, depth), BF16)] * 4,
        compiler_params=params(),
        cost_estimate=cost(count * depth, 6 * count * depth),
        name="split_sum",
    )(mine, first, second)


def down_body(*refs):
    left, right = refs[16:18]
    mirror = jnp.concatenate([ref[...].astype(F32) for ref in refs[18:-1]], axis=0)
    out = refs[-1]
    total = jnp.dot(left[...], stacked(refs[:8], CAP), preferred_element_type=F32)
    total += jnp.dot(right[...], stacked(refs[8:16], CAP), preferred_element_type=F32)
    out[...] = (total + mirror).astype(BF16)


def down_grads(arrivals, left, right, mirror):
    width, depth = left.shape[0], mirror[0].shape[1]
    whole = pl.BlockSpec(left.shape, lambda k: (0, 0))
    return pl.pallas_call(
        down_body,
        grid=(depth // BLOCK,),
        in_specs=[pl.BlockSpec((2 * CAP, BLOCK), lambda k: (0, k))] * 16
        + [whole, whole]
        + [pl.BlockSpec((part.shape[0], BLOCK), lambda k: (0, k)) for part in mirror],
        out_specs=pl.BlockSpec((width, BLOCK), lambda k: (0, k)),
        out_shape=jax.ShapeDtypeStruct((width, depth), BF16),
        compiler_params=params(),
        cost_estimate=cost(2 * 384 * depth * width, 2 * depth * (2 * width + 768)),
        name="down_grads",
    )(*arrivals, left, right, *mirror)


def combine_body(odd, plane, routes, first, direct, away, own, other, out, place):
    @pl.when(pl.program_id(0) == 0)
    def _():
        place[...] = one_hot_rows(plane, routes).T.astype(BF16)

    rows = jnp.concatenate([own[...].astype(F32), other[...].astype(F32)], axis=0).astype(BF16)
    added = jnp.dot(place[...], rows, preferred_element_type=F32)
    half = first.shape[0]
    out[:half] = (first[...].astype(F32) + added[:half]).astype(BF16)
    rest = jnp.where(odd[0] == 1, away[...].astype(F32), direct[...].astype(F32))
    out[half:] = (rest + added[half:]).astype(BF16)


def combine(odd, plane, routes, first, direct, away, own, other):
    half, depth = first.shape
    part = pl.BlockSpec((half, BLOCK), lambda k: (0, k))
    rows = pl.BlockSpec((CAP, BLOCK), lambda k: (0, k))
    return pl.pallas_call(
        combine_body,
        grid=(depth // BLOCK,),
        in_specs=[
            pl.BlockSpec(memory_space=pltpu.SMEM),
            pl.BlockSpec(memory_space=pltpu.SMEM),
            pl.BlockSpec(routes.shape, lambda k: (0, 0)),
            part,
            part,
            part,
            rows,
            rows,
        ],
        out_specs=pl.BlockSpec((2 * half, BLOCK), lambda k: (0, k)),
        out_shape=jax.ShapeDtypeStruct((2 * half, depth), BF16),
        scratch_shapes=[pltpu.VMEM((2 * half, 2 * CAP), BF16)],
        compiler_params=params(),
        cost_estimate=cost(4 * half * 48 * depth, 12 * half * depth),
        name="combine",
    )(odd, plane, routes, first, direct, away, own, other)


def after(value, *others):
    return lax.optimization_barrier((value, others))[0]


def go(rows, perm, axis="expert"):
    return lax.ppermute(rows, axis, perm)


def local(
    saved_input, grad_output, routes, route_weight, gate_weight, up_weight, down_weight, mirror_grad
):
    plane = (lax.axis_index("expert") // 8).astype(jnp.int32).reshape(1)
    odd = (lax.axis_index("pipe") % 2).astype(jnp.int32).reshape(1)
    weights = (gate_weight[0], up_weight[0], down_weight[0])
    pairs = [(s * 16 + e, ((s - 1) % 8) * 16 + (e ^ 8)) for s in range(8) for e in range(16)]

    behind_routes = go(after(routes[0].T, plane), BEHIND, "pipe")
    own, other, first, second = pick_rows(
        plane, routes[0].T, route_weight[0].T, saved_input[0], grad_output[0]
    )
    across = go(after(other, behind_routes), ACROSS)
    direct = go(second, ODD_BEHIND, "pipe")
    near = [own] + [go(own, along_x(by)) for by in OFFSETS]
    mirror = [go(after(mirror_grad[0], across, near[1], near[2]), MIRROR, "pipe")]
    near = [near[0]] + [after(part, across, direct) for part in near[1:]]
    away = go(after(second, across), AWAY_FIRST, "pipe")
    near = near + [go(part, SIBLING) for part in near]
    far = [after(across, *near[4:])]
    far = far + [go(far[0], along_x(by)) for by in OFFSETS]
    near[0] = after(near[0], *near[4:], away)
    near_mine, near_sibling, near_sibling_2, near_hidden = experts(near, *weights)
    far = [after(part, near_hidden) for part in far]
    near_sibling = after(near_sibling, *far)
    near_sibling_2 = after(near_sibling_2, near_sibling)
    near_parts = split_sum(near_mine, go(near_sibling, SIBLING), go(near_sibling_2, SIBLING))
    far = far + [go(part, SIBLING) for part in far]
    far[0] = after(far[0], near_parts, mirror[0])
    away = go(after(away, *far[4:]), AWAY_LAST, "pipe")
    near_back = [go(after(part, *far[4:]), along_x(-by)) for part, by in zip(near_parts[1:], OFFSETS)]
    far_mine, far_sibling, far_sibling_2, far_hidden = experts(far, *weights)
    near_back[0] = after(near_back[0], far_hidden)
    near_total = add_up(near_parts[0], near_back)
    first = go(after(first, near_parts), BEHIND, "pipe")
    far_sibling = after(far_sibling, near_total)
    far_sibling_2 = after(far_sibling_2, far_sibling)
    far_mine = after(far_mine, near_total)
    far_parts = split_sum(far_mine, go(far_sibling, SIBLING), go(far_sibling_2, SIBLING))
    far_back = [go(part, along_x(-by)) for part, by in zip(far_parts[1:], OFFSETS)]
    mirror[0] = after(mirror[0], far_hidden)
    down_grad = down_grads(near + far, near_hidden, far_hidden, mirror)
    far_total = add_up(after(far_parts[0], down_grad, away, first), far_back)
    near_back = go(near_total, BEHIND, "pipe")
    far_back = go(far_total, pairs, ("pipe", "expert"))
    back = combine(odd, plane, behind_routes, first, direct, away, near_back, far_back)
    return back[None], down_grad[None]


def add_up(first, others):
    total = first.astype(F32)
    for other in others:
        total = total + other.astype(F32)
    return total.astype(BF16)


def solution(mesh):
    in_specs = (
        P("pipe", "expert", None),
        P("pipe", "expert", None),
        P("pipe", "expert", None),
        P("pipe", "expert", None),
        P("pipe", None, "expert"),
        P("pipe", None, "expert"),
        P("pipe", "expert", None),
        P("pipe", "expert", None),
    )
    out_specs = (P("pipe", "expert", None), P("pipe", "expert", None))
    return jax.shard_map(local, mesh=mesh, in_specs=in_specs, out_specs=out_specs, check_vma=False)
```

```python
import functools

import jax
import jax.numpy as jnp
from jax import lax
from jax.experimental import pallas as pl
from jax.experimental.pallas import tpu as pltpu
from jax.sharding import PartitionSpec as P

CAP = 24
BLOCK = 3584
PICK_BLOCK = 1792
LIMIT = 48 * 1024 * 1024
F32 = jnp.float32
BF16 = jnp.bfloat16

BEHIND = [(i, (i - 1) % 8) for i in range(8)]
MIRROR = [(i, 7 - i) for i in range(8)]
ODD_BEHIND = [(i, i - 1) for i in range(1, 8, 2)]
AWAY_FIRST = [(0, 2), (2, 0), (4, 6), (6, 4)]
AWAY_LAST = [(2, 7), (6, 3), (0, 1), (4, 5)]
ACROSS = [(i, i ^ 8) for i in range(16)]
SIBLING = [(i, i ^ 1) for i in range(16)]


def along_x(by):
    return [(i, (i // 8) * 8 + ((i // 2 + by) % 4) * 2 + i % 2) for i in range(16)]


OFFSETS = (1, 3, 2)


def params(**kw):
    return pltpu.CompilerParams(vmem_limit_bytes=LIMIT, **kw)


def cost(flops, nbytes):
    return pl.CostEstimate(flops=flops, bytes_accessed=nbytes, transcendentals=0)


def one_hot_rows(plane, routes):
    tokens = routes.shape[1]
    chosen = routes[...]
    line = lax.broadcasted_iota(jnp.int32, (2 * CAP, tokens), 0)
    member = jnp.zeros((2 * CAP, tokens), F32)
    for j in range(2):
        expert = plane[0] if j == 0 else 1 - plane[0]
        named = jnp.max(jnp.where(chosen == expert, 1.0, 0.0), axis=0, keepdims=True)
        member = jnp.where(line >= CAP if j else line < CAP, named, member)
    row = lax.broadcasted_iota(jnp.int32, (tokens, tokens), 0)
    column = lax.broadcasted_iota(jnp.int32, (tokens, tokens), 1)
    upper = jnp.where(row <= column, 1.0, 0.0).astype(BF16)
    count = jnp.dot(member.astype(BF16), upper, preferred_element_type=F32)
    slot = jnp.where(line >= CAP, line - CAP, line).astype(F32)
    return jnp.where((count - 1.0 == slot) & (member > 0.0), 1.0, 0.0)


def pick_body(plane, routes, weight, saved, grad, own, other, first, second, one_hot, gain):
    tokens = routes.shape[1]

    @pl.when(pl.program_id(0) == 0)
    def _():
        hot = one_hot_rows(plane, routes)
        line = lax.broadcasted_iota(jnp.int32, (2 * CAP, tokens), 0)
        scale = jnp.zeros((2 * CAP, tokens), F32)
        for j in range(2):
            expert = plane[0] if j == 0 else 1 - plane[0]
            value = jnp.where(routes[...] == expert, weight[...], 0.0)
            value = jnp.sum(value, axis=0, keepdims=True)
            scale = jnp.where(line >= CAP if j else line < CAP, value, scale)
        one_hot[...] = hot.astype(BF16)
        total = jnp.sum(hot * scale, axis=1, keepdims=True)
        gain[...] = jnp.broadcast_to(total, gain.shape)

    pick = one_hot[...]
    grads = grad[...]
    rows = jnp.dot(pick, saved[...], preferred_element_type=F32)
    scaled = gain[:, :1] * jnp.dot(pick, grads, preferred_element_type=F32)
    own[...] = jnp.concatenate([rows[:CAP], scaled[:CAP]], axis=0).astype(BF16)
    other[...] = jnp.concatenate([rows[CAP:], scaled[CAP:]], axis=0).astype(BF16)
    first[...] = grads[: tokens // 2]
    second[...] = grads[tokens // 2 :]


def pick_rows(plane, routes, weight, saved, grad):
    tokens, depth = saved.shape
    whole = pl.BlockSpec(routes.shape, lambda k: (0, 0))
    tall = pl.BlockSpec((tokens, PICK_BLOCK), lambda k: (0, k))
    short = pl.BlockSpec((2 * CAP, PICK_BLOCK), lambda k: (0, k))
    half = pl.BlockSpec((tokens // 2, PICK_BLOCK), lambda k: (0, k))
    rows = jax.ShapeDtypeStruct((2 * CAP, depth), BF16)
    halves = jax.ShapeDtypeStruct((tokens // 2, depth), BF16)
    return pl.pallas_call(
        pick_body,
        grid=(depth // PICK_BLOCK,),
        in_specs=[pl.BlockSpec(memory_space=pltpu.SMEM), whole, whole, tall, tall],
        out_specs=[short, short, half, half],
        out_shape=[rows, rows, halves, halves],
        scratch_shapes=[pltpu.VMEM((2 * CAP, tokens), BF16), pltpu.VMEM((2 * CAP, 128), F32)],
        compiler_params=params(),
        cost_estimate=cost(4 * 48 * tokens * depth, 10 * tokens * depth),
        name="pick_rows",
    )(plane, routes, weight, saved, grad)


def stacked(refs, lower):
    parts = [ref[...].astype(F32)[lower : lower + CAP] for ref in refs]
    return jnp.concatenate(parts, axis=0).astype(BF16)


def contract_last(a, b):
    return lax.dot_general(a, b, (((1,), (1,)), ((), ())), preferred_element_type=F32)


def experts_body(steps, *refs):
    arrivals, (gate, up, down) = refs[:8], refs[8:11]
    mine, sibling, sibling_2, hidden_t = refs[11:15]
    gates, ups, pre_gate, pre_up, from_down, grad_gate, grad_up, arrived = refs[15:]
    step = pl.program_id(0)

    def fetch(i):
        rows = pl.ds(i * BLOCK, BLOCK)
        return (
            pltpu.make_async_copy(gate.at[rows], gates.at[i], arrived.at[0, i]),
            pltpu.make_async_copy(up.at[rows], ups.at[i], arrived.at[1, i]),
        )

    @pl.when(step == 0)
    def _():
        for i in range(steps):
            for copy in fetch(i):
                copy.start()
        pre_gate[...] = jnp.zeros_like(pre_gate)
        pre_up[...] = jnp.zeros_like(pre_up)
        from_down[...] = jnp.zeros_like(from_down)

    @pl.when(step < steps)
    def _():
        rows = stacked(arrivals, 0)
        scaled = stacked(arrivals, CAP)
        for copy in fetch(step):
            copy.wait()
        pre_gate[...] += jnp.dot(rows, gates[step], preferred_element_type=F32)
        pre_up[...] += jnp.dot(rows, ups[step], preferred_element_type=F32)
        from_down[...] += contract_last(scaled, down[...])

    @pl.when(step == steps)
    def _():
        value = pre_gate[...]
        sigma = 1.0 / (1.0 + jnp.exp(-value))
        activated = value * sigma
        slope = sigma * (1.0 + value * (1.0 - sigma))
        hidden_t[...] = (activated * pre_up[...]).T.astype(BF16)
        grad_gate[...] = (from_down[...] * pre_up[...] * slope).astype(BF16)
        grad_up[...] = (from_down[...] * activated).astype(BF16)

    @pl.when(step >= steps)
    def _():
        at = step - steps
        partial = contract_last(grad_gate[...], gates[at])
        partial = (partial + contract_last(grad_up[...], ups[at])).astype(BF16)
        half = partial.shape[0] // 2
        mine[...] = partial[:half]
        sibling[...] = partial[half : half + half // 2]
        sibling_2[...] = partial[half + half // 2 :]


def experts(arrivals, gate, up, down):
    depth, width = gate.shape
    steps = depth // BLOCK
    count = 8 * CAP

    def block(k):
        return jnp.minimum(k, steps - 1)

    def late(k):
        return jnp.maximum(k - steps, 0)

    out = pl.BlockSpec((count // 2, BLOCK), lambda k: (0, late(k)))
    half = pl.BlockSpec((count // 4, BLOCK), lambda k: (0, late(k)))
    sums = jax.ShapeDtypeStruct((count // 2, depth), BF16)
    halves = jax.ShapeDtypeStruct((count // 4, depth), BF16)
    return pl.pallas_call(
        functools.partial(experts_body, steps),
        grid=(2 * steps,),
        in_specs=[pl.BlockSpec((2 * CAP, BLOCK), lambda k: (0, block(k)))] * 8
        + [pl.BlockSpec(memory_space=pl.ANY)] * 2
        + [pl.BlockSpec((width, BLOCK), lambda k: (0, block(k)))],
        out_specs=[out, half, half, pl.BlockSpec((width, count), lambda k: (0, 0))],
        out_shape=[sums, halves, halves, jax.ShapeDtypeStruct((width, count), BF16)],
        scratch_shapes=[pltpu.VMEM((steps, BLOCK, width), BF16)] * 2
        + [pltpu.VMEM((count, width), F32)] * 3
        + [pltpu.VMEM((count, width), BF16)] * 2
        + [pltpu.SemaphoreType.DMA((2, steps))],
        compiler_params=params(),
        cost_estimate=cost(10 * count * depth * width, 2 * depth * (3 * width + 3 * count)),
        name="experts",
    )(*arrivals, gate, up, down)


def split_body(mine, first, second, *outs):
    theirs = jnp.concatenate([first[...].astype(F32), second[...].astype(F32)], axis=0)
    total = mine[...].astype(F32) + theirs
    for i, out in enumerate(outs):
        out[...] = total[i * CAP : (i + 1) * CAP].astype(BF16)


def split_sum(mine, first, second):
    count, depth = mine.shape
    spec = pl.BlockSpec((count, BLOCK), lambda k: (0, k))
    half = pl.BlockSpec((count // 2, BLOCK), lambda k: (0, k))
    out = pl.BlockSpec((CAP, BLOCK), lambda k: (0, k))
    return pl.pallas_call(
        split_body,
        grid=(depth // BLOCK,),
        in_specs=[spec, half, half],
        out_specs=[out] * 4,
        out_shape=[jax.ShapeDtypeStruct((CAP, depth), BF16)] * 4,
        compiler_params=params(),
        cost_estimate=cost(count * depth, 6 * count * depth),
        name="split_sum",
    )(mine, first, second)


def down_body(*refs):
    left, right = refs[16:18]
    mirror = jnp.concatenate([ref[...].astype(F32) for ref in refs[18:-1]], axis=0)
    out = refs[-1]
    total = jnp.dot(left[...], stacked(refs[:8], CAP), preferred_element_type=F32)
    total += jnp.dot(right[...], stacked(refs[8:16], CAP), preferred_element_type=F32)
    out[...] = (total + mirror).astype(BF16)


def down_grads(arrivals, left, right, mirror):
    width, depth = left.shape[0], mirror[0].shape[1]
    whole = pl.BlockSpec(left.shape, lambda k: (0, 0))
    return pl.pallas_call(
        down_body,
        grid=(depth // BLOCK,),
        in_specs=[pl.BlockSpec((2 * CAP, BLOCK), lambda k: (0, k))] * 16
        + [whole, whole]
        + [pl.BlockSpec((part.shape[0], BLOCK), lambda k: (0, k)) for part in mirror],
        out_specs=pl.BlockSpec((width, BLOCK), lambda k: (0, k)),
        out_shape=jax.ShapeDtypeStruct((width, depth), BF16),
        compiler_params=params(),
        cost_estimate=cost(2 * 384 * depth * width, 2 * depth * (2 * width + 768)),
        name="down_grads",
    )(*arrivals, left, right, *mirror)


def combine_body(odd, plane, routes, first, direct, away, own, other, out, place):
    @pl.when(pl.program_id(0) == 0)
    def _():
        place[...] = one_hot_rows(plane, routes).T.astype(BF16)

    rows = jnp.concatenate([own[...].astype(F32), other[...].astype(F32)], axis=0).astype(BF16)
    added = jnp.dot(place[...], rows, preferred_element_type=F32)
    half = first.shape[0]
    out[:half] = (first[...].astype(F32) + added[:half]).astype(BF16)
    rest = jnp.where(odd[0] == 1, away[...].astype(F32), direct[...].astype(F32))
    out[half:] = (rest + added[half:]).astype(BF16)


def combine(odd, plane, routes, first, direct, away, own, other):
    half, depth = first.shape
    part = pl.BlockSpec((half, BLOCK), lambda k: (0, k))
    rows = pl.BlockSpec((CAP, BLOCK), lambda k: (0, k))
    return pl.pallas_call(
        combine_body,
        grid=(depth // BLOCK,),
        in_specs=[
            pl.BlockSpec(memory_space=pltpu.SMEM),
            pl.BlockSpec(memory_space=pltpu.SMEM),
            pl.BlockSpec(routes.shape, lambda k: (0, 0)),
            part,
            part,
            part,
            rows,
            rows,
        ],
        out_specs=pl.BlockSpec((2 * half, BLOCK), lambda k: (0, k)),
        out_shape=jax.ShapeDtypeStruct((2 * half, depth), BF16),
        scratch_shapes=[pltpu.VMEM((2 * half, 2 * CAP), BF16)],
        compiler_params=params(),
        cost_estimate=cost(4 * half * 48 * depth, 12 * half * depth),
        name="combine",
    )(odd, plane, routes, first, direct, away, own, other)


def after(value, *others):
    return lax.optimization_barrier((value, others))[0]


def go(rows, perm, axis="expert"):
    return lax.ppermute(rows, axis, perm)


def local(
    saved_input, grad_output, routes, route_weight, gate_weight, up_weight, down_weight, mirror_grad
):
    plane = (lax.axis_index("expert") // 8).astype(jnp.int32).reshape(1)
    odd = (lax.axis_index("pipe") % 2).astype(jnp.int32).reshape(1)
    weights = (gate_weight[0], up_weight[0], down_weight[0])
    pairs = [(s * 16 + e, ((s - 1) % 8) * 16 + (e ^ 8)) for s in range(8) for e in range(16)]

    behind_routes = go(after(routes[0].T, plane), BEHIND, "pipe")
    own, other, first, second = pick_rows(
        plane, routes[0].T, route_weight[0].T, saved_input[0], grad_output[0]
    )
    across = go(after(other, behind_routes), ACROSS)
    direct = go(second, ODD_BEHIND, "pipe")
    away = go(second, AWAY_FIRST, "pipe")
    near = [own] + [go(own, along_x(by)) for by in OFFSETS]
    mirror = after(mirror_grad[0], across, near[1], near[2])
    mirror = [go(mirror, MIRROR, "pipe")]
    near = [near[0]] + [after(part, across) for part in near[1:3]] + [after(near[3], across, direct, away)]
    near = near + [go(part, SIBLING) for part in near]
    far = [after(across, *near[4:])]
    far = far + [go(far[0], along_x(by)) for by in OFFSETS]
    near[0] = after(near[0], *near[4:])
    near_mine, near_sibling, near_sibling_2, near_hidden = experts(near, *weights)
    far = [after(part, near_hidden) for part in far]
    near_sibling = after(near_sibling, *far)
    near_sibling_2 = after(near_sibling_2, near_sibling)
    near_parts = split_sum(near_mine, go(near_sibling, SIBLING), go(near_sibling_2, SIBLING))
    far = far + [go(part, SIBLING) for part in far]
    far[0] = after(far[0], near_parts, mirror[0])
    away = go(away, AWAY_LAST, "pipe")
    near_back = [go(after(part, *far[4:]), along_x(-by)) for part, by in zip(near_parts[1:], OFFSETS)]
    far_mine, far_sibling, far_sibling_2, far_hidden = experts(far, *weights)
    near_back[0] = after(near_back[0], far_hidden)
    near_total = add_up(near_parts[0], near_back)
    first = go(after(first, *near[4:]), BEHIND, "pipe")
    far_sibling = after(far_sibling, near_total)
    far_sibling_2 = after(far_sibling_2, far_sibling)
    far_mine = after(far_mine, near_total)
    far_parts = split_sum(far_mine, go(far_sibling, SIBLING), go(far_sibling_2, SIBLING))
    far_back = [go(part, along_x(-by)) for part, by in zip(far_parts[1:], OFFSETS)]
    mirror[0] = after(mirror[0], far_hidden, away)
    down_grad = down_grads(near + far, near_hidden, far_hidden, mirror)
    far_total = add_up(after(far_parts[0], down_grad, first), far_back)
    near_back = go(near_total, BEHIND, "pipe")
    far_back = go(far_total, pairs, ("pipe", "expert"))
    back = combine(odd, plane, behind_routes, first, direct, away, near_back, far_back)
    return back[None], down_grad[None]


def add_up(first, others):
    total = first.astype(F32)
    for other in others:
        total = total + other.astype(F32)
    return total.astype(BF16)


def solution(mesh):
    in_specs = (
        P("pipe", "expert", None),
        P("pipe", "expert", None),
        P("pipe", "expert", None),
        P("pipe", "expert", None),
        P("pipe", None, "expert"),
        P("pipe", None, "expert"),
        P("pipe", "expert", None),
        P("pipe", "expert", None),
    )
    out_specs = (P("pipe", "expert", None), P("pipe", "expert", None))
    return jax.shard_map(local, mesh=mesh, in_specs=in_specs, out_specs=out_specs, check_vma=False)
```

```python
import functools

import jax
import jax.numpy as jnp
from jax import lax
from jax.experimental import pallas as pl
from jax.experimental.pallas import tpu as pltpu
from jax.sharding import PartitionSpec as P

CAP = 24
BLOCK = 3584
PICK_BLOCK = 1792
DIRECT = 96
TURNED = 144
LIMIT = 48 * 1024 * 1024
F32 = jnp.float32
BF16 = jnp.bfloat16

BEHIND = [(i, (i - 1) % 8) for i in range(8)]
MIRROR = [(i, 7 - i) for i in range(8)]
ODD_BEHIND = [(i, i - 1) for i in range(1, 8, 2)]
AWAY_FIRST = [(0, 2), (2, 0), (4, 6), (6, 4)]
AWAY_LAST = [(2, 7), (6, 3), (0, 1), (4, 5)]
DOWN_Z = [(i, i // 4 * 4 + (i - 1) % 4) for i in range(8)]
CROSS_Y = [(3, 7), (7, 3)]
ACROSS = [(i, i ^ 8) for i in range(16)]
SIBLING = [(i, i ^ 1) for i in range(16)]


def along_x(by):
    return [(i, (i // 8) * 8 + ((i // 2 + by) % 4) * 2 + i % 2) for i in range(16)]


OFFSETS = (1, 3, 2)


def params(**kw):
    return pltpu.CompilerParams(vmem_limit_bytes=LIMIT, **kw)


def cost(flops, nbytes):
    return pl.CostEstimate(flops=flops, bytes_accessed=nbytes, transcendentals=0)


def one_hot_rows(plane, routes):
    tokens = routes.shape[1]
    chosen = routes[...]
    line = lax.broadcasted_iota(jnp.int32, (2 * CAP, tokens), 0)
    member = jnp.zeros((2 * CAP, tokens), F32)
    for j in range(2):
        expert = plane[0] if j == 0 else 1 - plane[0]
        named = jnp.max(jnp.where(chosen == expert, 1.0, 0.0), axis=0, keepdims=True)
        member = jnp.where(line >= CAP if j else line < CAP, named, member)
    row = lax.broadcasted_iota(jnp.int32, (tokens, tokens), 0)
    column = lax.broadcasted_iota(jnp.int32, (tokens, tokens), 1)
    upper = jnp.where(row <= column, 1.0, 0.0).astype(BF16)
    count = jnp.dot(member.astype(BF16), upper, preferred_element_type=F32)
    slot = jnp.where(line >= CAP, line - CAP, line).astype(F32)
    return jnp.where((count - 1.0 == slot) & (member > 0.0), 1.0, 0.0)


def pick_body(
    plane, routes, weight, saved, grad, own, other, first, second, third, one_hot, gain
):
    tokens = routes.shape[1]

    @pl.when(pl.program_id(0) == 0)
    def _():
        hot = one_hot_rows(plane, routes)
        line = lax.broadcasted_iota(jnp.int32, (2 * CAP, tokens), 0)
        scale = jnp.zeros((2 * CAP, tokens), F32)
        for j in range(2):
            expert = plane[0] if j == 0 else 1 - plane[0]
            value = jnp.where(routes[...] == expert, weight[...], 0.0)
            value = jnp.sum(value, axis=0, keepdims=True)
            scale = jnp.where(line >= CAP if j else line < CAP, value, scale)
        one_hot[...] = hot.astype(BF16)
        total = jnp.sum(hot * scale, axis=1, keepdims=True)
        gain[...] = jnp.broadcast_to(total, gain.shape)

    pick = one_hot[...]
    grads = grad[...]
    rows = jnp.dot(pick, saved[...], preferred_element_type=F32)
    scaled = gain[:, :1] * jnp.dot(pick, grads, preferred_element_type=F32)
    own[...] = jnp.concatenate([rows[:CAP], scaled[:CAP]], axis=0).astype(BF16)
    other[...] = jnp.concatenate([rows[CAP:], scaled[CAP:]], axis=0).astype(BF16)
    first[...] = grads[:DIRECT]
    second[...] = grads[DIRECT:TURNED]
    third[...] = grads[TURNED:]


def pick_rows(plane, routes, weight, saved, grad):
    tokens, depth = saved.shape
    whole = pl.BlockSpec(routes.shape, lambda k: (0, 0))
    tall = pl.BlockSpec((tokens, PICK_BLOCK), lambda k: (0, k))
    short = pl.BlockSpec((2 * CAP, PICK_BLOCK), lambda k: (0, k))
    direct = pl.BlockSpec((DIRECT, PICK_BLOCK), lambda k: (0, k))
    turned = pl.BlockSpec((TURNED - DIRECT, PICK_BLOCK), lambda k: (0, k))
    rest = pl.BlockSpec((tokens - TURNED, PICK_BLOCK), lambda k: (0, k))
    rows = jax.ShapeDtypeStruct((2 * CAP, depth), BF16)
    return pl.pallas_call(
        pick_body,
        grid=(depth // PICK_BLOCK,),
        in_specs=[pl.BlockSpec(memory_space=pltpu.SMEM), whole, whole, tall, tall],
        out_specs=[short, short, direct, turned, rest],
        out_shape=[
            rows,
            rows,
            jax.ShapeDtypeStruct((DIRECT, depth), BF16),
            jax.ShapeDtypeStruct((TURNED - DIRECT, depth), BF16),
            jax.ShapeDtypeStruct((tokens - TURNED, depth), BF16),
        ],
        scratch_shapes=[pltpu.VMEM((2 * CAP, tokens), BF16), pltpu.VMEM((2 * CAP, 128), F32)],
        compiler_params=params(),
        cost_estimate=cost(4 * 48 * tokens * depth, 10 * tokens * depth),
        name="pick_rows",
    )(plane, routes, weight, saved, grad)


def stacked(refs, lower):
    parts = [ref[...].astype(F32)[lower : lower + CAP] for ref in refs]
    return jnp.concatenate(parts, axis=0).astype(BF16)


def contract_last(a, b):
    return lax.dot_general(a, b, (((1,), (1,)), ((), ())), preferred_element_type=F32)


def experts_body(steps, *refs):
    arrivals, (gate, up, down) = refs[:8], refs[8:11]
    mine, sibling, sibling_2, hidden_t = refs[11:15]
    gates, ups, pre_gate, pre_up, from_down, grad_gate, grad_up, arrived = refs[15:]
    step = pl.program_id(0)

    def fetch(i):
        rows = pl.ds(i * BLOCK, BLOCK)
        return (
            pltpu.make_async_copy(gate.at[rows], gates.at[i], arrived.at[0, i]),
            pltpu.make_async_copy(up.at[rows], ups.at[i], arrived.at[1, i]),
        )

    @pl.when(step == 0)
    def _():
        for i in range(steps):
            for copy in fetch(i):
                copy.start()
        pre_gate[...] = jnp.zeros_like(pre_gate)
        pre_up[...] = jnp.zeros_like(pre_up)
        from_down[...] = jnp.zeros_like(from_down)

    @pl.when(step < steps)
    def _():
        rows = stacked(arrivals, 0)
        scaled = stacked(arrivals, CAP)
        for copy in fetch(step):
            copy.wait()
        pre_gate[...] += jnp.dot(rows, gates[step], preferred_element_type=F32)
        pre_up[...] += jnp.dot(rows, ups[step], preferred_element_type=F32)
        from_down[...] += contract_last(scaled, down[...])

    @pl.when(step == steps)
    def _():
        value = pre_gate[...]
        sigma = 1.0 / (1.0 + jnp.exp(-value))
        activated = value * sigma
        slope = sigma * (1.0 + value * (1.0 - sigma))
        hidden_t[...] = (activated * pre_up[...]).T.astype(BF16)
        grad_gate[...] = (from_down[...] * pre_up[...] * slope).astype(BF16)
        grad_up[...] = (from_down[...] * activated).astype(BF16)

    @pl.when(step >= steps)
    def _():
        at = step - steps
        partial = contract_last(grad_gate[...], gates[at])
        partial = (partial + contract_last(grad_up[...], ups[at])).astype(BF16)
        half = partial.shape[0] // 2
        mine[...] = partial[:half]
        sibling[...] = partial[half : half + half // 2]
        sibling_2[...] = partial[half + half // 2 :]


def experts(arrivals, gate, up, down):
    depth, width = gate.shape
    steps = depth // BLOCK
    count = 8 * CAP

    def block(k):
        return jnp.minimum(k, steps - 1)

    def late(k):
        return jnp.maximum(k - steps, 0)

    out = pl.BlockSpec((count // 2, BLOCK), lambda k: (0, late(k)))
    half = pl.BlockSpec((count // 4, BLOCK), lambda k: (0, late(k)))
    sums = jax.ShapeDtypeStruct((count // 2, depth), BF16)
    halves = jax.ShapeDtypeStruct((count // 4, depth), BF16)
    return pl.pallas_call(
        functools.partial(experts_body, steps),
        grid=(2 * steps,),
        in_specs=[pl.BlockSpec((2 * CAP, BLOCK), lambda k: (0, block(k)))] * 8
        + [pl.BlockSpec(memory_space=pl.ANY)] * 2
        + [pl.BlockSpec((width, BLOCK), lambda k: (0, block(k)))],
        out_specs=[out, half, half, pl.BlockSpec((width, count), lambda k: (0, 0))],
        out_shape=[sums, halves, halves, jax.ShapeDtypeStruct((width, count), BF16)],
        scratch_shapes=[pltpu.VMEM((steps, BLOCK, width), BF16)] * 2
        + [pltpu.VMEM((count, width), F32)] * 3
        + [pltpu.VMEM((count, width), BF16)] * 2
        + [pltpu.SemaphoreType.DMA((2, steps))],
        compiler_params=params(),
        cost_estimate=cost(10 * count * depth * width, 2 * depth * (3 * width + 3 * count)),
        name="experts",
    )(*arrivals, gate, up, down)


def split_body(mine, first, second, *outs):
    theirs = jnp.concatenate([first[...].astype(F32), second[...].astype(F32)], axis=0)
    total = mine[...].astype(F32) + theirs
    for i, out in enumerate(outs):
        out[...] = total[i * CAP : (i + 1) * CAP].astype(BF16)


def split_sum(mine, first, second):
    count, depth = mine.shape
    spec = pl.BlockSpec((count, BLOCK), lambda k: (0, k))
    half = pl.BlockSpec((count // 2, BLOCK), lambda k: (0, k))
    out = pl.BlockSpec((CAP, BLOCK), lambda k: (0, k))
    return pl.pallas_call(
        split_body,
        grid=(depth // BLOCK,),
        in_specs=[spec, half, half],
        out_specs=[out] * 4,
        out_shape=[jax.ShapeDtypeStruct((CAP, depth), BF16)] * 4,
        compiler_params=params(),
        cost_estimate=cost(count * depth, 6 * count * depth),
        name="split_sum",
    )(mine, first, second)


def down_body(*refs):
    left, right = refs[16:18]
    mirror = jnp.concatenate([ref[...].astype(F32) for ref in refs[18:-1]], axis=0)
    out = refs[-1]
    total = jnp.dot(left[...], stacked(refs[:8], CAP), preferred_element_type=F32)
    total += jnp.dot(right[...], stacked(refs[8:16], CAP), preferred_element_type=F32)
    out[...] = (total + mirror).astype(BF16)


def down_grads(arrivals, left, right, mirror):
    width, depth = left.shape[0], mirror[0].shape[1]
    whole = pl.BlockSpec(left.shape, lambda k: (0, 0))
    return pl.pallas_call(
        down_body,
        grid=(depth // BLOCK,),
        in_specs=[pl.BlockSpec((2 * CAP, BLOCK), lambda k: (0, k))] * 16
        + [whole, whole]
        + [pl.BlockSpec((part.shape[0], BLOCK), lambda k: (0, k)) for part in mirror],
        out_specs=pl.BlockSpec((width, BLOCK), lambda k: (0, k)),
        out_shape=jax.ShapeDtypeStruct((width, depth), BF16),
        compiler_params=params(),
        cost_estimate=cost(2 * 384 * depth * width, 2 * depth * (2 * width + 768)),
        name="down_grads",
    )(*arrivals, left, right, *mirror)


def combine_body(
    rank, plane, routes, first, turned, crossed, direct, away, own, other, out, place
):
    @pl.when(pl.program_id(0) == 0)
    def _():
        place[...] = one_hot_rows(plane, routes).T.astype(BF16)

    rows = jnp.concatenate([own[...].astype(F32), other[...].astype(F32)], axis=0).astype(BF16)
    added = jnp.dot(place[...], rows, preferred_element_type=F32)
    last = lax.rem(rank[0], 4) == 3
    odd = lax.rem(rank[0], 2) == 1
    second = jnp.where(last, crossed[...].astype(F32), turned[...].astype(F32))
    third = jnp.where(odd, away[...].astype(F32), direct[...].astype(F32))
    out[:DIRECT] = (first[...].astype(F32) + added[:DIRECT]).astype(BF16)
    out[DIRECT:TURNED] = (second + added[DIRECT:TURNED]).astype(BF16)
    out[TURNED:] = (third + added[TURNED:]).astype(BF16)


def combine(rank, plane, routes, *parts):
    tokens, depth = routes.shape[1], parts[0].shape[1]
    return pl.pallas_call(
        combine_body,
        grid=(depth // BLOCK,),
        in_specs=[
            pl.BlockSpec(memory_space=pltpu.SMEM),
            pl.BlockSpec(memory_space=pltpu.SMEM),
            pl.BlockSpec(routes.shape, lambda k: (0, 0)),
        ]
        + [pl.BlockSpec((part.shape[0], BLOCK), lambda k: (0, k)) for part in parts],
        out_specs=pl.BlockSpec((tokens, BLOCK), lambda k: (0, k)),
        out_shape=jax.ShapeDtypeStruct((tokens, depth), BF16),
        scratch_shapes=[pltpu.VMEM((tokens, 2 * CAP), BF16)],
        compiler_params=params(),
        cost_estimate=cost(2 * tokens * 48 * depth, 6 * tokens * depth),
        name="combine",
    )(rank, plane, routes, *parts)


def after(value, *others):
    return lax.optimization_barrier((value, others))[0]


def go(rows, perm, axis="expert"):
    return lax.ppermute(rows, axis, perm)


def local(
    saved_input, grad_output, routes, route_weight, gate_weight, up_weight, down_weight, mirror_grad
):
    plane = (lax.axis_index("expert") // 8).astype(jnp.int32).reshape(1)
    rank = lax.axis_index("pipe").astype(jnp.int32).reshape(1)
    weights = (gate_weight[0], up_weight[0], down_weight[0])
    pairs = [(s * 16 + e, ((s - 1) % 8) * 16 + (e ^ 8)) for s in range(8) for e in range(16)]

    behind_routes = go(after(routes[0].T, plane), BEHIND, "pipe")
    own, other, first, second, third = pick_rows(
        plane, routes[0].T, route_weight[0].T, saved_input[0], grad_output[0]
    )
    across = go(after(other, behind_routes), ACROSS)
    turned = go(second, DOWN_Z, "pipe")
    away = go(third, AWAY_FIRST, "pipe")
    near = [own] + [go(own, along_x(by)) for by in OFFSETS]
    mirror = after(mirror_grad[0], across, near[1], near[2], turned, away)
    mirror = [go(mirror, MIRROR, "pipe")]
    near = [near[0]] + [after(part, across) for part in near[1:]]
    near = near + [go(part, SIBLING) for part in near]
    far = [after(across, *near[4:])]
    far = far + [go(far[0], along_x(by)) for by in OFFSETS]
    near[0] = after(near[0], *near[4:])
    direct = go(after(third, *near[4:]), ODD_BEHIND, "pipe")
    near_mine, near_sibling, near_sibling_2, near_hidden = experts(near, *weights)
    far = [after(part, near_hidden) for part in far]
    near_sibling = after(near_sibling, *far, direct)
    near_sibling_2 = after(near_sibling_2, near_sibling)
    near_parts = split_sum(near_mine, go(near_sibling, SIBLING), go(near_sibling_2, SIBLING))
    far = far + [go(part, SIBLING) for part in far]
    far[0] = after(far[0], near_parts, mirror[0])
    away = go(away, AWAY_LAST, "pipe")
    near_back = [go(after(part, *far[4:]), along_x(-by)) for part, by in zip(near_parts[1:], OFFSETS)]
    far_mine, far_sibling, far_sibling_2, far_hidden = experts(far, *weights)
    near_back[0] = after(near_back[0], far_hidden)
    near_total = add_up(near_parts[0], near_back)
    first = go(after(first, *near[4:]), BEHIND, "pipe")
    crossed = go(after(turned, far_hidden, mirror[0]), CROSS_Y, "pipe")
    far_sibling = after(far_sibling, near_total)
    far_sibling_2 = after(far_sibling_2, far_sibling)
    far_mine = after(far_mine, near_total, away)
    far_parts = split_sum(far_mine, go(far_sibling, SIBLING), go(far_sibling_2, SIBLING))
    far_back = [go(part, along_x(-by)) for part, by in zip(far_parts[1:], OFFSETS)]
    mirror[0] = after(mirror[0], far_hidden)
    down_grad = down_grads(near + far, near_hidden, far_hidden, mirror)
    far_total = add_up(after(far_parts[0], down_grad, first, crossed), far_back)
    near_back = go(near_total, BEHIND, "pipe")
    far_back = go(far_total, pairs, ("pipe", "expert"))
    back = combine(
        rank, plane, behind_routes, first, turned, crossed, direct, away, near_back, far_back
    )
    return back[None], down_grad[None]


def add_up(first, others):
    total = first.astype(F32)
    for other in others:
        total = total + other.astype(F32)
    return total.astype(BF16)


def solution(mesh):
    in_specs = (
        P("pipe", "expert", None),
        P("pipe", "expert", None),
        P("pipe", "expert", None),
        P("pipe", "expert", None),
        P("pipe", None, "expert"),
        P("pipe", None, "expert"),
        P("pipe", "expert", None),
        P("pipe", "expert", None),
    )
    out_specs = (P("pipe", "expert", None), P("pipe", "expert", None))
    return jax.shard_map(local, mesh=mesh, in_specs=in_specs, out_specs=out_specs, check_vma=False)
```

```python
import functools

import jax
import jax.numpy as jnp
from jax import lax
from jax.experimental import pallas as pl
from jax.experimental.pallas import tpu as pltpu
from jax.sharding import PartitionSpec as P

CAP = 24
BLOCK = 3584
PICK_BLOCK = 1792
RISE_BLOCK = 3584
DIRECT = 96
TURNED = 144
LIMIT = 48 * 1024 * 1024
F32 = jnp.float32
BF16 = jnp.bfloat16

BEHIND = [(i, (i - 1) % 8) for i in range(8)]
MIRROR = [(i, 7 - i) for i in range(8)]
ODD_BEHIND = [(i, i - 1) for i in range(1, 8, 2)]
AWAY_FIRST = [(0, 2), (2, 0), (4, 6), (6, 4)]
AWAY_LAST = [(2, 7), (6, 3), (0, 1), (4, 5)]
DOWN_Z = [(i, i // 4 * 4 + (i - 1) % 4) for i in range(8)]
CROSS_Y = [(3, 7), (7, 3)]
ACROSS = [(i, i ^ 8) for i in range(16)]
SIBLING = [(i, i ^ 1) for i in range(16)]


def along_x(by):
    return [(i, (i // 8) * 8 + ((i // 2 + by) % 4) * 2 + i % 2) for i in range(16)]


OFFSETS = (1, 3, 2)


def params(**kw):
    return pltpu.CompilerParams(vmem_limit_bytes=LIMIT, **kw)


def cost(flops, nbytes):
    return pl.CostEstimate(flops=flops, bytes_accessed=nbytes, transcendentals=0)


def one_hot_rows(plane, routes):
    tokens = routes.shape[1]
    chosen = routes[...]
    line = lax.broadcasted_iota(jnp.int32, (2 * CAP, tokens), 0)
    member = jnp.zeros((2 * CAP, tokens), F32)
    for j in range(2):
        expert = plane[0] if j == 0 else 1 - plane[0]
        named = jnp.max(jnp.where(chosen == expert, 1.0, 0.0), axis=0, keepdims=True)
        member = jnp.where(line >= CAP if j else line < CAP, named, member)
    row = lax.broadcasted_iota(jnp.int32, (tokens, tokens), 0)
    column = lax.broadcasted_iota(jnp.int32, (tokens, tokens), 1)
    upper = jnp.where(row <= column, 1.0, 0.0).astype(BF16)
    count = jnp.dot(member.astype(BF16), upper, preferred_element_type=F32)
    slot = jnp.where(line >= CAP, line - CAP, line).astype(F32)
    return jnp.where((count - 1.0 == slot) & (member > 0.0), 1.0, 0.0)


def pick_body(
    plane, routes, weight, saved, grad, own, other, first, second, third, one_hot, gain
):
    tokens = routes.shape[1]

    @pl.when(pl.program_id(0) == 0)
    def _():
        hot = one_hot_rows(plane, routes)
        line = lax.broadcasted_iota(jnp.int32, (2 * CAP, tokens), 0)
        scale = jnp.zeros((2 * CAP, tokens), F32)
        for j in range(2):
            expert = plane[0] if j == 0 else 1 - plane[0]
            value = jnp.where(routes[...] == expert, weight[...], 0.0)
            value = jnp.sum(value, axis=0, keepdims=True)
            scale = jnp.where(line >= CAP if j else line < CAP, value, scale)
        one_hot[...] = hot.astype(BF16)
        total = jnp.sum(hot * scale, axis=1, keepdims=True)
        gain[...] = jnp.broadcast_to(total, gain.shape)

    pick = one_hot[...]
    grads = grad[...]
    rows = jnp.dot(pick, saved[...], preferred_element_type=F32)
    scaled = gain[:, :1] * jnp.dot(pick, grads, preferred_element_type=F32)
    own[...] = jnp.concatenate([rows[:CAP], scaled[:CAP]], axis=0).astype(BF16)
    other[...] = jnp.concatenate([rows[CAP:], scaled[CAP:]], axis=0).astype(BF16)
    first[...] = grads[:DIRECT]
    second[...] = grads[DIRECT:TURNED]
    third[...] = grads[TURNED:]


def pick_rows(plane, routes, weight, saved, grad):
    tokens, depth = saved.shape
    whole = pl.BlockSpec(routes.shape, lambda k: (0, 0))
    tall = pl.BlockSpec((tokens, PICK_BLOCK), lambda k: (0, k))
    short = pl.BlockSpec((2 * CAP, PICK_BLOCK), lambda k: (0, k))
    direct = pl.BlockSpec((DIRECT, PICK_BLOCK), lambda k: (0, k))
    turned = pl.BlockSpec((TURNED - DIRECT, PICK_BLOCK), lambda k: (0, k))
    rest = pl.BlockSpec((tokens - TURNED, PICK_BLOCK), lambda k: (0, k))
    rows = jax.ShapeDtypeStruct((2 * CAP, depth), BF16)
    return pl.pallas_call(
        pick_body,
        grid=(depth // PICK_BLOCK,),
        in_specs=[pl.BlockSpec(memory_space=pltpu.SMEM), whole, whole, tall, tall],
        out_specs=[short, short, direct, turned, rest],
        out_shape=[
            rows,
            rows,
            jax.ShapeDtypeStruct((DIRECT, depth), BF16),
            jax.ShapeDtypeStruct((TURNED - DIRECT, depth), BF16),
            jax.ShapeDtypeStruct((tokens - TURNED, depth), BF16),
        ],
        scratch_shapes=[pltpu.VMEM((2 * CAP, tokens), BF16), pltpu.VMEM((2 * CAP, 128), F32)],
        compiler_params=params(),
        cost_estimate=cost(4 * 48 * tokens * depth, 10 * tokens * depth),
        name="pick_rows",
    )(plane, routes, weight, saved, grad)


def stacked(refs, lower):
    parts = [ref[...].astype(F32)[lower : lower + CAP] for ref in refs]
    return jnp.concatenate(parts, axis=0).astype(BF16)


def contract_last(a, b):
    return lax.dot_general(a, b, (((1,), (1,)), ((), ())), preferred_element_type=F32)


def experts_body(steps, *refs):
    arrivals, (gate, up, down) = refs[:8], refs[8:11]
    mine, sibling, sibling_2, hidden_t = refs[11:15]
    gates, ups, pre_gate, pre_up, from_down, grad_gate, grad_up, arrived = refs[15:]
    step = pl.program_id(0)

    def fetch(i):
        rows = pl.ds(i * BLOCK, BLOCK)
        return (
            pltpu.make_async_copy(gate.at[rows], gates.at[i], arrived.at[0, i]),
            pltpu.make_async_copy(up.at[rows], ups.at[i], arrived.at[1, i]),
        )

    @pl.when(step == 0)
    def _():
        for i in range(steps):
            for copy in fetch(i):
                copy.start()
        pre_gate[...] = jnp.zeros_like(pre_gate)
        pre_up[...] = jnp.zeros_like(pre_up)
        from_down[...] = jnp.zeros_like(from_down)

    @pl.when(step < steps)
    def _():
        rows = stacked(arrivals, 0)
        scaled = stacked(arrivals, CAP)
        for copy in fetch(step):
            copy.wait()
        pre_gate[...] += jnp.dot(rows, gates[step], preferred_element_type=F32)
        pre_up[...] += jnp.dot(rows, ups[step], preferred_element_type=F32)
        from_down[...] += contract_last(scaled, down[...])

    @pl.when(step == steps)
    def _():
        value = pre_gate[...]
        sigma = 1.0 / (1.0 + jnp.exp(-value))
        activated = value * sigma
        slope = sigma * (1.0 + value * (1.0 - sigma))
        hidden_t[...] = (activated * pre_up[...]).T.astype(BF16)
        grad_gate[...] = (from_down[...] * pre_up[...] * slope).astype(BF16)
        grad_up[...] = (from_down[...] * activated).astype(BF16)

    @pl.when(step >= steps)
    def _():
        at = step - steps
        partial = contract_last(grad_gate[...], gates[at])
        partial = (partial + contract_last(grad_up[...], ups[at])).astype(BF16)
        half = partial.shape[0] // 2
        mine[...] = partial[:half]
        sibling[...] = partial[half : half + half // 2]
        sibling_2[...] = partial[half + half // 2 :]


def experts(arrivals, gate, up, down):
    depth, width = gate.shape
    steps = depth // BLOCK
    count = 8 * CAP

    def block(k):
        return jnp.minimum(k, steps - 1)

    def late(k):
        return jnp.maximum(k - steps, 0)

    out = pl.BlockSpec((count // 2, BLOCK), lambda k: (0, late(k)))
    half = pl.BlockSpec((count // 4, BLOCK), lambda k: (0, late(k)))
    sums = jax.ShapeDtypeStruct((count // 2, depth), BF16)
    halves = jax.ShapeDtypeStruct((count // 4, depth), BF16)
    return pl.pallas_call(
        functools.partial(experts_body, steps),
        grid=(2 * steps,),
        in_specs=[pl.BlockSpec((2 * CAP, BLOCK), lambda k: (0, block(k)))] * 8
        + [pl.BlockSpec(memory_space=pl.ANY)] * 2
        + [pl.BlockSpec((width, BLOCK), lambda k: (0, block(k)))],
        out_specs=[out, half, half, pl.BlockSpec((width, count), lambda k: (0, 0))],
        out_shape=[sums, halves, halves, jax.ShapeDtypeStruct((width, count), BF16)],
        scratch_shapes=[pltpu.VMEM((steps, BLOCK, width), BF16)] * 2
        + [pltpu.VMEM((count, width), F32)] * 3
        + [pltpu.VMEM((count, width), BF16)] * 2
        + [pltpu.SemaphoreType.DMA((2, steps))],
        compiler_params=params(),
        cost_estimate=cost(10 * count * depth * width, 2 * depth * (3 * width + 3 * count)),
        name="experts",
    )(*arrivals, gate, up, down)


def rise_body(steps, *refs):
    arrivals, (gate, up, down) = refs[:8], refs[8:11]
    hidden_t, grad_gate, grad_up = refs[11:14]
    pre_gate, pre_up, from_down = refs[14:]
    step = pl.program_id(0)
    rows = stacked(arrivals, 0)
    scaled = stacked(arrivals, CAP)
    gates = jnp.dot(rows, gate[...], preferred_element_type=F32)
    ups = jnp.dot(rows, up[...], preferred_element_type=F32)
    downs = contract_last(scaled, down[...])

    @pl.when(step == 0)
    def _():
        pre_gate[...] = gates
        pre_up[...] = ups
        from_down[...] = downs

    @pl.when(step > 0)
    def _():
        pre_gate[...] += gates
        pre_up[...] += ups
        from_down[...] += downs

    @pl.when(step == steps - 1)
    def _():
        value = pre_gate[...]
        sigma = 1.0 / (1.0 + jnp.exp(-value))
        activated = value * sigma
        slope = sigma * (1.0 + value * (1.0 - sigma))
        hidden_t[...] = (activated * pre_up[...]).T.astype(BF16)
        grad_gate[...] = (from_down[...] * pre_up[...] * slope).astype(BF16)
        grad_up[...] = (from_down[...] * activated).astype(BF16)


def rise(arrivals, gate, up, down):
    depth, width = gate.shape
    count = 8 * CAP
    steps = depth // RISE_BLOCK
    flat = pl.BlockSpec((count, width), lambda k: (0, 0))
    grads = jax.ShapeDtypeStruct((count, width), BF16)
    return pl.pallas_call(
        functools.partial(rise_body, steps),
        grid=(steps,),
        in_specs=[pl.BlockSpec((2 * CAP, RISE_BLOCK), lambda k: (0, k))] * 8
        + [pl.BlockSpec((RISE_BLOCK, width), lambda k: (k, 0))] * 2
        + [pl.BlockSpec((width, RISE_BLOCK), lambda k: (0, k))],
        out_specs=[pl.BlockSpec((width, count), lambda k: (0, 0)), flat, flat],
        out_shape=[jax.ShapeDtypeStruct((width, count), BF16), grads, grads],
        scratch_shapes=[pltpu.VMEM((count, width), F32)] * 3,
        compiler_params=params(),
        cost_estimate=cost(0, 0),
        name="rise",
    )(*arrivals, gate, up, down)


def fall_body(grad_gate, grad_up, gate, up, mine, sibling, sibling_2):
    partial = contract_last(grad_gate[...], gate[...])
    partial = (partial + contract_last(grad_up[...], up[...])).astype(BF16)
    half = partial.shape[0] // 2
    mine[...] = partial[:half]
    sibling[...] = partial[half : half + half // 2]
    sibling_2[...] = partial[half + half // 2 :]


def fall(grad_gate, grad_up, gate, up):
    depth, width = gate.shape
    count = grad_gate.shape[0]
    flat = pl.BlockSpec((count, width), lambda k: (0, 0))
    tall = pl.BlockSpec((RISE_BLOCK, width), lambda k: (k, 0))
    out = pl.BlockSpec((count // 2, RISE_BLOCK), lambda k: (0, k))
    half = pl.BlockSpec((count // 4, RISE_BLOCK), lambda k: (0, k))
    halves = jax.ShapeDtypeStruct((count // 4, depth), BF16)
    return pl.pallas_call(
        fall_body,
        grid=(depth // RISE_BLOCK,),
        in_specs=[flat, flat, tall, tall],
        out_specs=[out, half, half],
        out_shape=[jax.ShapeDtypeStruct((count // 2, depth), BF16), halves, halves],
        compiler_params=params(),
        cost_estimate=cost(4 * count * depth * width, 2 * depth * (2 * width + count)),
        name="fall",
    )(grad_gate, grad_up, gate, up)


def split_body(mine, first, second, *outs):
    theirs = jnp.concatenate([first[...].astype(F32), second[...].astype(F32)], axis=0)
    total = mine[...].astype(F32) + theirs
    for i, out in enumerate(outs):
        out[...] = total[i * CAP : (i + 1) * CAP].astype(BF16)


def split_sum(mine, first, second):
    count, depth = mine.shape
    spec = pl.BlockSpec((count, BLOCK), lambda k: (0, k))
    half = pl.BlockSpec((count // 2, BLOCK), lambda k: (0, k))
    out = pl.BlockSpec((CAP, BLOCK), lambda k: (0, k))
    return pl.pallas_call(
        split_body,
        grid=(depth // BLOCK,),
        in_specs=[spec, half, half],
        out_specs=[out] * 4,
        out_shape=[jax.ShapeDtypeStruct((CAP, depth), BF16)] * 4,
        compiler_params=params(),
        cost_estimate=cost(count * depth, 6 * count * depth),
        name="split_sum",
    )(mine, first, second)


def down_body(*refs):
    left, right = refs[16:18]
    mirror = jnp.concatenate([ref[...].astype(F32) for ref in refs[18:-1]], axis=0)
    out = refs[-1]
    total = jnp.dot(left[...], stacked(refs[:8], CAP), preferred_element_type=F32)
    total += jnp.dot(right[...], stacked(refs[8:16], CAP), preferred_element_type=F32)
    out[...] = (total + mirror).astype(BF16)


def down_grads(arrivals, left, right, mirror):
    width, depth = left.shape[0], mirror[0].shape[1]
    whole = pl.BlockSpec(left.shape, lambda k: (0, 0))
    return pl.pallas_call(
        down_body,
        grid=(depth // BLOCK,),
        in_specs=[pl.BlockSpec((2 * CAP, BLOCK), lambda k: (0, k))] * 16
        + [whole, whole]
        + [pl.BlockSpec((part.shape[0], BLOCK), lambda k: (0, k)) for part in mirror],
        out_specs=pl.BlockSpec((width, BLOCK), lambda k: (0, k)),
        out_shape=jax.ShapeDtypeStruct((width, depth), BF16),
        compiler_params=params(),
        cost_estimate=cost(2 * 384 * depth * width, 2 * depth * (2 * width + 768)),
        name="down_grads",
    )(*arrivals, left, right, *mirror)


def combine_body(
    rank, plane, routes, first, turned, crossed, direct, away, own, other, out, place
):
    @pl.when(pl.program_id(0) == 0)
    def _():
        place[...] = one_hot_rows(plane, routes).T.astype(BF16)

    rows = jnp.concatenate([own[...].astype(F32), other[...].astype(F32)], axis=0).astype(BF16)
    added = jnp.dot(place[...], rows, preferred_element_type=F32)
    last = lax.rem(rank[0], 4) == 3
    odd = lax.rem(rank[0], 2) == 1
    second = jnp.where(last, crossed[...].astype(F32), turned[...].astype(F32))
    third = jnp.where(odd, away[...].astype(F32), direct[...].astype(F32))
    out[:DIRECT] = (first[...].astype(F32) + added[:DIRECT]).astype(BF16)
    out[DIRECT:TURNED] = (second + added[DIRECT:TURNED]).astype(BF16)
    out[TURNED:] = (third + added[TURNED:]).astype(BF16)


def combine(rank, plane, routes, *parts):
    tokens, depth = routes.shape[1], parts[0].shape[1]
    return pl.pallas_call(
        combine_body,
        grid=(depth // BLOCK,),
        in_specs=[
            pl.BlockSpec(memory_space=pltpu.SMEM),
            pl.BlockSpec(memory_space=pltpu.SMEM),
            pl.BlockSpec(routes.shape, lambda k: (0, 0)),
        ]
        + [pl.BlockSpec((part.shape[0], BLOCK), lambda k: (0, k)) for part in parts],
        out_specs=pl.BlockSpec((tokens, BLOCK), lambda k: (0, k)),
        out_shape=jax.ShapeDtypeStruct((tokens, depth), BF16),
        scratch_shapes=[pltpu.VMEM((tokens, 2 * CAP), BF16)],
        compiler_params=params(),
        cost_estimate=cost(2 * tokens * 48 * depth, 6 * tokens * depth),
        name="combine",
    )(rank, plane, routes, *parts)


def after(value, *others):
    return lax.optimization_barrier((value, others))[0]


def go(rows, perm, axis="expert"):
    return lax.ppermute(rows, axis, perm)


def local(
    saved_input, grad_output, routes, route_weight, gate_weight, up_weight, down_weight, mirror_grad
):
    plane = (lax.axis_index("expert") // 8).astype(jnp.int32).reshape(1)
    rank = lax.axis_index("pipe").astype(jnp.int32).reshape(1)
    weights = (gate_weight[0], up_weight[0], down_weight[0])
    pairs = [(s * 16 + e, ((s - 1) % 8) * 16 + (e ^ 8)) for s in range(8) for e in range(16)]

    behind_routes = go(after(routes[0].T, plane), BEHIND, "pipe")
    own, other, first, second, third = pick_rows(
        plane, routes[0].T, route_weight[0].T, saved_input[0], grad_output[0]
    )
    across = go(after(other, behind_routes), ACROSS)
    turned = go(second, DOWN_Z, "pipe")
    away = go(third, AWAY_FIRST, "pipe")
    near = [own] + [go(own, along_x(by)) for by in OFFSETS]
    mirror = after(mirror_grad[0], across, near[1], near[2], turned, away)
    mirror = [go(mirror, MIRROR, "pipe")]
    near = [near[0]] + [after(part, across) for part in near[1:]]
    near = near + [go(part, SIBLING) for part in near]
    far = [after(across, *near[4:])]
    far = far + [go(far[0], along_x(by)) for by in OFFSETS]
    near[0] = after(near[0], *near[4:])
    direct = go(after(third, *near[4:]), ODD_BEHIND, "pipe")
    near_mine, near_sibling, near_sibling_2, near_hidden = experts(near, *weights)
    far = [after(part, near_hidden) for part in far]
    near_sibling = after(near_sibling, *far, direct)
    near_sibling_2 = after(near_sibling_2, near_sibling)
    near_parts = split_sum(near_mine, go(near_sibling, SIBLING), go(near_sibling_2, SIBLING))
    far = far + [go(part, SIBLING) for part in far]
    far[0] = after(far[0], near_parts)
    away = go(away, AWAY_LAST, "pipe")
    near_back = [go(after(part, *far[4:]), along_x(-by)) for part, by in zip(near_parts[1:], OFFSETS)]
    far_hidden, grad_gate, grad_up = rise(far, *weights)
    grad_gate = after(grad_gate, mirror[0])
    far_mine, far_sibling, far_sibling_2 = fall(grad_gate, grad_up, *weights[:2])
    near_back[0] = after(near_back[0], far_mine)
    near_total = add_up(near_parts[0], near_back)
    first = go(after(first, *near[4:]), BEHIND, "pipe")
    crossed = go(after(turned, far_hidden, mirror[0]), CROSS_Y, "pipe")
    far_sibling = after(far_sibling, near_total)
    far_sibling_2 = after(far_sibling_2, far_sibling)
    far_mine = after(far_mine, near_total, away)
    far_parts = split_sum(far_mine, go(far_sibling, SIBLING), go(far_sibling_2, SIBLING))
    far_back = [go(part, along_x(-by)) for part, by in zip(far_parts[1:], OFFSETS)]
    mirror[0] = after(mirror[0], far_hidden)
    down_grad = down_grads(near + far, near_hidden, far_hidden, mirror)
    far_total = add_up(after(far_parts[0], down_grad, first, crossed), far_back)
    near_back = go(near_total, BEHIND, "pipe")
    far_back = go(far_total, pairs, ("pipe", "expert"))
    back = combine(
        rank, plane, behind_routes, first, turned, crossed, direct, away, near_back, far_back
    )
    return back[None], down_grad[None]


def add_up(first, others):
    total = first.astype(F32)
    for other in others:
        total = total + other.astype(F32)
    return total.astype(BF16)


def solution(mesh):
    in_specs = (
        P("pipe", "expert", None),
        P("pipe", "expert", None),
        P("pipe", "expert", None),
        P("pipe", "expert", None),
        P("pipe", None, "expert"),
        P("pipe", None, "expert"),
        P("pipe", "expert", None),
        P("pipe", "expert", None),
    )
    out_specs = (P("pipe", "expert", None), P("pipe", "expert", None))
    return jax.shard_map(local, mesh=mesh, in_specs=in_specs, out_specs=out_specs, check_vma=False)
```

```python
import functools

import jax
import jax.numpy as jnp
from jax import lax
from jax.experimental import pallas as pl
from jax.experimental.pallas import tpu as pltpu
from jax.sharding import PartitionSpec as P

CAP = 24
BLOCK = 3584
PICK_BLOCK = 1792
RISE_BLOCK = 3584
DIRECT = 80
TURNED = 144
LIMIT = 48 * 1024 * 1024
F32 = jnp.float32
BF16 = jnp.bfloat16

BEHIND = [(i, (i - 1) % 8) for i in range(8)]
MIRROR = [(i, 7 - i) for i in range(8)]
ODD_BEHIND = [(i, i - 1) for i in range(1, 8, 2)]
AWAY_FIRST = [(0, 2), (2, 0), (4, 6), (6, 4)]
AWAY_LAST = [(2, 7), (6, 3), (0, 1), (4, 5)]
DOWN_Z = [(i, i // 4 * 4 + (i - 1) % 4) for i in range(8)]
CROSS_Y = [(3, 7), (7, 3)]
ACROSS = [(i, i ^ 8) for i in range(16)]
SIBLING = [(i, i ^ 1) for i in range(16)]


def along_x(by):
    return [(i, (i // 8) * 8 + ((i // 2 + by) % 4) * 2 + i % 2) for i in range(16)]


OFFSETS = (1, 3, 2)


def params(**kw):
    return pltpu.CompilerParams(vmem_limit_bytes=LIMIT, **kw)


def cost(flops, nbytes):
    return pl.CostEstimate(flops=flops, bytes_accessed=nbytes, transcendentals=0)


def one_hot_rows(plane, routes):
    tokens = routes.shape[1]
    chosen = routes[...]
    line = lax.broadcasted_iota(jnp.int32, (2 * CAP, tokens), 0)
    member = jnp.zeros((2 * CAP, tokens), F32)
    for j in range(2):
        expert = plane[0] if j == 0 else 1 - plane[0]
        named = jnp.max(jnp.where(chosen == expert, 1.0, 0.0), axis=0, keepdims=True)
        member = jnp.where(line >= CAP if j else line < CAP, named, member)
    row = lax.broadcasted_iota(jnp.int32, (tokens, tokens), 0)
    column = lax.broadcasted_iota(jnp.int32, (tokens, tokens), 1)
    upper = jnp.where(row <= column, 1.0, 0.0).astype(BF16)
    count = jnp.dot(member.astype(BF16), upper, preferred_element_type=F32)
    slot = jnp.where(line >= CAP, line - CAP, line).astype(F32)
    return jnp.where((count - 1.0 == slot) & (member > 0.0), 1.0, 0.0)


def pick_body(
    plane, routes, weight, saved, grad, own, other, first, second, third, one_hot, gain
):
    tokens = routes.shape[1]

    @pl.when(pl.program_id(0) == 0)
    def _():
        hot = one_hot_rows(plane, routes)
        line = lax.broadcasted_iota(jnp.int32, (2 * CAP, tokens), 0)
        scale = jnp.zeros((2 * CAP, tokens), F32)
        for j in range(2):
            expert = plane[0] if j == 0 else 1 - plane[0]
            value = jnp.where(routes[...] == expert, weight[...], 0.0)
            value = jnp.sum(value, axis=0, keepdims=True)
            scale = jnp.where(line >= CAP if j else line < CAP, value, scale)
        one_hot[...] = hot.astype(BF16)
        total = jnp.sum(hot * scale, axis=1, keepdims=True)
        gain[...] = jnp.broadcast_to(total, gain.shape)

    pick = one_hot[...]
    grads = grad[...]
    rows = jnp.dot(pick, saved[...], preferred_element_type=F32)
    scaled = gain[:, :1] * jnp.dot(pick, grads, preferred_element_type=F32)
    own[...] = jnp.concatenate([rows[:CAP], scaled[:CAP]], axis=0).astype(BF16)
    other[...] = jnp.concatenate([rows[CAP:], scaled[CAP:]], axis=0).astype(BF16)
    first[...] = grads[:DIRECT]
    second[...] = grads[DIRECT:TURNED]
    third[...] = grads[TURNED:]


def pick_rows(plane, routes, weight, saved, grad):
    tokens, depth = saved.shape
    whole = pl.BlockSpec(routes.shape, lambda k: (0, 0))
    tall = pl.BlockSpec((tokens, PICK_BLOCK), lambda k: (0, k))
    short = pl.BlockSpec((2 * CAP, PICK_BLOCK), lambda k: (0, k))
    direct = pl.BlockSpec((DIRECT, PICK_BLOCK), lambda k: (0, k))
    turned = pl.BlockSpec((TURNED - DIRECT, PICK_BLOCK), lambda k: (0, k))
    rest = pl.BlockSpec((tokens - TURNED, PICK_BLOCK), lambda k: (0, k))
    rows = jax.ShapeDtypeStruct((2 * CAP, depth), BF16)
    return pl.pallas_call(
        pick_body,
        grid=(depth // PICK_BLOCK,),
        in_specs=[pl.BlockSpec(memory_space=pltpu.SMEM), whole, whole, tall, tall],
        out_specs=[short, short, direct, turned, rest],
        out_shape=[
            rows,
            rows,
            jax.ShapeDtypeStruct((DIRECT, depth), BF16),
            jax.ShapeDtypeStruct((TURNED - DIRECT, depth), BF16),
            jax.ShapeDtypeStruct((tokens - TURNED, depth), BF16),
        ],
        scratch_shapes=[pltpu.VMEM((2 * CAP, tokens), BF16), pltpu.VMEM((2 * CAP, 128), F32)],
        compiler_params=params(),
        cost_estimate=cost(4 * 48 * tokens * depth, 10 * tokens * depth),
        name="pick_rows",
    )(plane, routes, weight, saved, grad)


def stacked(refs, lower):
    parts = [ref[...].astype(F32)[lower : lower + CAP] for ref in refs]
    return jnp.concatenate(parts, axis=0).astype(BF16)


def contract_last(a, b):
    return lax.dot_general(a, b, (((1,), (1,)), ((), ())), preferred_element_type=F32)


def experts_body(steps, *refs):
    arrivals, (gate, up, down) = refs[:8], refs[8:11]
    mine, sibling, sibling_2, hidden_t = refs[11:15]
    gates, ups, pre_gate, pre_up, from_down, grad_gate, grad_up, arrived = refs[15:]
    step = pl.program_id(0)

    def fetch(i):
        rows = pl.ds(i * BLOCK, BLOCK)
        return (
            pltpu.make_async_copy(gate.at[rows], gates.at[i], arrived.at[0, i]),
            pltpu.make_async_copy(up.at[rows], ups.at[i], arrived.at[1, i]),
        )

    @pl.when(step == 0)
    def _():
        for i in range(steps):
            for copy in fetch(i):
                copy.start()
        pre_gate[...] = jnp.zeros_like(pre_gate)
        pre_up[...] = jnp.zeros_like(pre_up)
        from_down[...] = jnp.zeros_like(from_down)

    @pl.when(step < steps)
    def _():
        rows = stacked(arrivals, 0)
        scaled = stacked(arrivals, CAP)
        for copy in fetch(step):
            copy.wait()
        pre_gate[...] += jnp.dot(rows, gates[step], preferred_element_type=F32)
        pre_up[...] += jnp.dot(rows, ups[step], preferred_element_type=F32)
        from_down[...] += contract_last(scaled, down[...])

    @pl.when(step == steps)
    def _():
        value = pre_gate[...]
        sigma = 1.0 / (1.0 + jnp.exp(-value))
        activated = value * sigma
        slope = sigma * (1.0 + value * (1.0 - sigma))
        hidden_t[...] = (activated * pre_up[...]).T.astype(BF16)
        grad_gate[...] = (from_down[...] * pre_up[...] * slope).astype(BF16)
        grad_up[...] = (from_down[...] * activated).astype(BF16)

    @pl.when(step >= steps)
    def _():
        at = step - steps
        partial = contract_last(grad_gate[...], gates[at])
        partial = (partial + contract_last(grad_up[...], ups[at])).astype(BF16)
        half = partial.shape[0] // 2
        mine[...] = partial[:half]
        sibling[...] = partial[half : half + half // 2]
        sibling_2[...] = partial[half + half // 2 :]


def experts(arrivals, gate, up, down):
    depth, width = gate.shape
    steps = depth // BLOCK
    count = 8 * CAP

    def block(k):
        return jnp.minimum(k, steps - 1)

    def late(k):
        return jnp.maximum(k - steps, 0)

    out = pl.BlockSpec((count // 2, BLOCK), lambda k: (0, late(k)))
    half = pl.BlockSpec((count // 4, BLOCK), lambda k: (0, late(k)))
    sums = jax.ShapeDtypeStruct((count // 2, depth), BF16)
    halves = jax.ShapeDtypeStruct((count // 4, depth), BF16)
    return pl.pallas_call(
        functools.partial(experts_body, steps),
        grid=(2 * steps,),
        in_specs=[pl.BlockSpec((2 * CAP, BLOCK), lambda k: (0, block(k)))] * 8
        + [pl.BlockSpec(memory_space=pl.ANY)] * 2
        + [pl.BlockSpec((width, BLOCK), lambda k: (0, block(k)))],
        out_specs=[out, half, half, pl.BlockSpec((width, count), lambda k: (0, 0))],
        out_shape=[sums, halves, halves, jax.ShapeDtypeStruct((width, count), BF16)],
        scratch_shapes=[pltpu.VMEM((steps, BLOCK, width), BF16)] * 2
        + [pltpu.VMEM((count, width), F32)] * 3
        + [pltpu.VMEM((count, width), BF16)] * 2
        + [pltpu.SemaphoreType.DMA((2, steps))],
        compiler_params=params(),
        cost_estimate=cost(10 * count * depth * width, 2 * depth * (3 * width + 3 * count)),
        name="experts",
    )(*arrivals, gate, up, down)


def rise_body(steps, *refs):
    arrivals, (gate, up, down) = refs[:8], refs[8:11]
    hidden_t, grad_gate, grad_up = refs[11:14]
    pre_gate, pre_up, from_down = refs[14:]
    step = pl.program_id(0)
    rows = stacked(arrivals, 0)
    scaled = stacked(arrivals, CAP)
    gates = jnp.dot(rows, gate[...], preferred_element_type=F32)
    ups = jnp.dot(rows, up[...], preferred_element_type=F32)
    downs = contract_last(scaled, down[...])

    @pl.when(step == 0)
    def _():
        pre_gate[...] = gates
        pre_up[...] = ups
        from_down[...] = downs

    @pl.when(step > 0)
    def _():
        pre_gate[...] += gates
        pre_up[...] += ups
        from_down[...] += downs

    @pl.when(step == steps - 1)
    def _():
        value = pre_gate[...]
        sigma = 1.0 / (1.0 + jnp.exp(-value))
        activated = value * sigma
        slope = sigma * (1.0 + value * (1.0 - sigma))
        hidden_t[...] = (activated * pre_up[...]).T.astype(BF16)
        grad_gate[...] = (from_down[...] * pre_up[...] * slope).astype(BF16)
        grad_up[...] = (from_down[...] * activated).astype(BF16)


def rise(arrivals, gate, up, down):
    depth, width = gate.shape
    count = 8 * CAP
    steps = depth // RISE_BLOCK
    flat = pl.BlockSpec((count, width), lambda k: (0, 0))
    grads = jax.ShapeDtypeStruct((count, width), BF16)
    return pl.pallas_call(
        functools.partial(rise_body, steps),
        grid=(steps,),
        in_specs=[pl.BlockSpec((2 * CAP, RISE_BLOCK), lambda k: (0, k))] * 8
        + [pl.BlockSpec((RISE_BLOCK, width), lambda k: (k, 0))] * 2
        + [pl.BlockSpec((width, RISE_BLOCK), lambda k: (0, k))],
        out_specs=[pl.BlockSpec((width, count), lambda k: (0, 0)), flat, flat],
        out_shape=[jax.ShapeDtypeStruct((width, count), BF16), grads, grads],
        scratch_shapes=[pltpu.VMEM((count, width), F32)] * 3,
        compiler_params=params(),
        cost_estimate=cost(0, 0),
        name="rise",
    )(*arrivals, gate, up, down)


def fall_body(grad_gate, grad_up, gate, up, mine, sibling, sibling_2):
    partial = contract_last(grad_gate[...], gate[...])
    partial = (partial + contract_last(grad_up[...], up[...])).astype(BF16)
    half = partial.shape[0] // 2
    mine[...] = partial[:half]
    sibling[...] = partial[half : half + half // 2]
    sibling_2[...] = partial[half + half // 2 :]


def fall(grad_gate, grad_up, gate, up):
    depth, width = gate.shape
    count = grad_gate.shape[0]
    flat = pl.BlockSpec((count, width), lambda k: (0, 0))
    tall = pl.BlockSpec((RISE_BLOCK, width), lambda k: (k, 0))
    out = pl.BlockSpec((count // 2, RISE_BLOCK), lambda k: (0, k))
    half = pl.BlockSpec((count // 4, RISE_BLOCK), lambda k: (0, k))
    halves = jax.ShapeDtypeStruct((count // 4, depth), BF16)
    return pl.pallas_call(
        fall_body,
        grid=(depth // RISE_BLOCK,),
        in_specs=[flat, flat, tall, tall],
        out_specs=[out, half, half],
        out_shape=[jax.ShapeDtypeStruct((count // 2, depth), BF16), halves, halves],
        compiler_params=params(),
        cost_estimate=cost(4 * count * depth * width, 2 * depth * (2 * width + count)),
        name="fall",
    )(grad_gate, grad_up, gate, up)


def split_body(mine, first, second, *outs):
    theirs = jnp.concatenate([first[...].astype(F32), second[...].astype(F32)], axis=0)
    total = mine[...].astype(F32) + theirs
    for i, out in enumerate(outs):
        out[...] = total[i * CAP : (i + 1) * CAP].astype(BF16)


def split_sum(mine, first, second):
    count, depth = mine.shape
    spec = pl.BlockSpec((count, BLOCK), lambda k: (0, k))
    half = pl.BlockSpec((count // 2, BLOCK), lambda k: (0, k))
    out = pl.BlockSpec((CAP, BLOCK), lambda k: (0, k))
    return pl.pallas_call(
        split_body,
        grid=(depth // BLOCK,),
        in_specs=[spec, half, half],
        out_specs=[out] * 4,
        out_shape=[jax.ShapeDtypeStruct((CAP, depth), BF16)] * 4,
        compiler_params=params(),
        cost_estimate=cost(count * depth, 6 * count * depth),
        name="split_sum",
    )(mine, first, second)


def down_body(*refs):
    left, right = refs[16:18]
    mirror = jnp.concatenate([ref[...].astype(F32) for ref in refs[18:-1]], axis=0)
    out = refs[-1]
    total = jnp.dot(left[...], stacked(refs[:8], CAP), preferred_element_type=F32)
    total += jnp.dot(right[...], stacked(refs[8:16], CAP), preferred_element_type=F32)
    out[...] = (total + mirror).astype(BF16)


def down_grads(arrivals, left, right, mirror):
    width, depth = left.shape[0], mirror[0].shape[1]
    whole = pl.BlockSpec(left.shape, lambda k: (0, 0))
    return pl.pallas_call(
        down_body,
        grid=(depth // BLOCK,),
        in_specs=[pl.BlockSpec((2 * CAP, BLOCK), lambda k: (0, k))] * 16
        + [whole, whole]
        + [pl.BlockSpec((part.shape[0], BLOCK), lambda k: (0, k)) for part in mirror],
        out_specs=pl.BlockSpec((width, BLOCK), lambda k: (0, k)),
        out_shape=jax.ShapeDtypeStruct((width, depth), BF16),
        compiler_params=params(),
        cost_estimate=cost(2 * 384 * depth * width, 2 * depth * (2 * width + 768)),
        name="down_grads",
    )(*arrivals, left, right, *mirror)


def combine_body(
    rank, plane, routes, first, turned, crossed, direct, away, own, other, out, place
):
    @pl.when(pl.program_id(0) == 0)
    def _():
        place[...] = one_hot_rows(plane, routes).T.astype(BF16)

    rows = jnp.concatenate([own[...].astype(F32), other[...].astype(F32)], axis=0).astype(BF16)
    added = jnp.dot(place[...], rows, preferred_element_type=F32)
    last = lax.rem(rank[0], 4) == 3
    odd = lax.rem(rank[0], 2) == 1
    second = jnp.where(last, crossed[...].astype(F32), turned[...].astype(F32))
    third = jnp.where(odd, away[...].astype(F32), direct[...].astype(F32))
    out[:DIRECT] = (first[...].astype(F32) + added[:DIRECT]).astype(BF16)
    out[DIRECT:TURNED] = (second + added[DIRECT:TURNED]).astype(BF16)
    out[TURNED:] = (third + added[TURNED:]).astype(BF16)


def combine(rank, plane, routes, *parts):
    tokens, depth = routes.shape[1], parts[0].shape[1]
    return pl.pallas_call(
        combine_body,
        grid=(depth // BLOCK,),
        in_specs=[
            pl.BlockSpec(memory_space=pltpu.SMEM),
            pl.BlockSpec(memory_space=pltpu.SMEM),
            pl.BlockSpec(routes.shape, lambda k: (0, 0)),
        ]
        + [pl.BlockSpec((part.shape[0], BLOCK), lambda k: (0, k)) for part in parts],
        out_specs=pl.BlockSpec((tokens, BLOCK), lambda k: (0, k)),
        out_shape=jax.ShapeDtypeStruct((tokens, depth), BF16),
        scratch_shapes=[pltpu.VMEM((tokens, 2 * CAP), BF16)],
        compiler_params=params(),
        cost_estimate=cost(2 * tokens * 48 * depth, 6 * tokens * depth),
        name="combine",
    )(rank, plane, routes, *parts)


def after(value, *others):
    return lax.optimization_barrier((value, others))[0]


def go(rows, perm, axis="expert"):
    return lax.ppermute(rows, axis, perm)


def local(
    saved_input, grad_output, routes, route_weight, gate_weight, up_weight, down_weight, mirror_grad
):
    plane = (lax.axis_index("expert") // 8).astype(jnp.int32).reshape(1)
    rank = lax.axis_index("pipe").astype(jnp.int32).reshape(1)
    weights = (gate_weight[0], up_weight[0], down_weight[0])
    pairs = [(s * 16 + e, ((s - 1) % 8) * 16 + (e ^ 8)) for s in range(8) for e in range(16)]

    behind_routes = go(after(routes[0].T, plane), BEHIND, "pipe")
    own, other, first, second, third = pick_rows(
        plane, routes[0].T, route_weight[0].T, saved_input[0], grad_output[0]
    )
    across = go(after(other, behind_routes), ACROSS)
    turned = go(second, DOWN_Z, "pipe")
    away = go(third, AWAY_FIRST, "pipe")
    near = [own] + [go(own, along_x(by)) for by in OFFSETS]
    mirror = after(mirror_grad[0], across, near[1], near[2], turned, away)
    mirror = [go(mirror, MIRROR, "pipe")]
    near = [near[0]] + [after(part, across) for part in near[1:]]
    near = near + [go(part, SIBLING) for part in near]
    far = [after(across, *near[4:])]
    far = far + [go(far[0], along_x(by)) for by in OFFSETS]
    near[0] = after(near[0], *near[4:])
    direct = go(after(third, *near[4:]), ODD_BEHIND, "pipe")
    near_mine, near_sibling, near_sibling_2, near_hidden = experts(near, *weights)
    far = [after(part, near_hidden) for part in far]
    near_sibling = after(near_sibling, *far, direct)
    near_sibling_2 = after(near_sibling_2, near_sibling)
    near_parts = split_sum(near_mine, go(near_sibling, SIBLING), go(near_sibling_2, SIBLING))
    far = far + [go(part, SIBLING) for part in far]
    far[0] = after(far[0], near_parts)
    away = go(away, AWAY_LAST, "pipe")
    near_back = [go(after(part, *far[4:]), along_x(-by)) for part, by in zip(near_parts[1:], OFFSETS)]
    far_hidden, grad_gate, grad_up = rise(far, *weights)
    grad_gate = after(grad_gate, mirror[0])
    far_mine, far_sibling, far_sibling_2 = fall(grad_gate, grad_up, *weights[:2])
    near_back[0] = after(near_back[0], far_mine)
    near_total = add_up(near_parts[0], near_back)
    first = go(after(first, *near[4:]), BEHIND, "pipe")
    crossed = go(after(turned, far_hidden, mirror[0]), CROSS_Y, "pipe")
    far_sibling = after(far_sibling, near_total)
    far_sibling_2 = after(far_sibling_2, far_sibling)
    far_mine = after(far_mine, near_total, away)
    far_parts = split_sum(far_mine, go(far_sibling, SIBLING), go(far_sibling_2, SIBLING))
    far_back = [go(part, along_x(-by)) for part, by in zip(far_parts[1:], OFFSETS)]
    mirror[0] = after(mirror[0], far_hidden)
    down_grad = down_grads(near + far, near_hidden, far_hidden, mirror)
    far_total = add_up(after(far_parts[0], down_grad, first, crossed), far_back)
    near_back = go(near_total, BEHIND, "pipe")
    far_back = go(far_total, pairs, ("pipe", "expert"))
    back = combine(
        rank, plane, behind_routes, first, turned, crossed, direct, away, near_back, far_back
    )
    return back[None], down_grad[None]


def add_up(first, others):
    total = first.astype(F32)
    for other in others:
        total = total + other.astype(F32)
    return total.astype(BF16)


def solution(mesh):
    in_specs = (
        P("pipe", "expert", None),
        P("pipe", "expert", None),
        P("pipe", "expert", None),
        P("pipe", "expert", None),
        P("pipe", None, "expert"),
        P("pipe", None, "expert"),
        P("pipe", "expert", None),
        P("pipe", "expert", None),
    )
    out_specs = (P("pipe", "expert", None), P("pipe", "expert", None))
    return jax.shard_map(local, mesh=mesh, in_specs=in_specs, out_specs=out_specs, check_vma=False)
```
